256 devices in a mesh: grp: 8 (over y, core), dev: 32 (over z, x).
Axes of the slice: x: 4, y: 4, z: 8, core: 2. Of those that a mesh axis runs over, the one named last changes fastest.
Arguments:
- multipoles: bfloat16 [9, 32, 65536], P(None, None, ('grp', 'dev')), may hold values from -6 to 6
- harmonics: bfloat16 [121, 32, 65536], P(None, None, ('grp', 'dev')), may hold values from -6 to 6
- positions: float32 [3, 32, 65536], P(None, None, ('grp', 'dev')), may hold values from -3 to 3
- atom_counts: int32 [65536], P(('grp', 'dev')), may hold values from 16 to 32
- source_ops: float32 [9, 121, 121], replicated, may hold values from -0.1875 to 0.1875
- field_ops: float32 [9, 121, 121], replicated, may hold values from -0.5 to 0.5
- m2l_ops: bfloat16 [316, 121, 121], replicated, may hold values from -0.03125 to 0.03125
- send_list: int32 [256, 256, 4], P(('grp', 'dev')), may hold values from -1 to 255, as said below
- m2l_list: int32 [316, 65536], P(None, ('grp', 'dev')), may hold values from -1 to 1279, as said below
- near_list: int32 [27, 65536], P(None, ('grp', 'dev')), may hold values from -1 to 287, as said below
Outputs:
- fields: float32 [9, 32, 65536], P(None, None, ('grp', 'dev'))
The draws below stay inside these ranges and needn't reach their ends.
Inputs may be any that keep to these rules, and one draw needn't show every extreme that they name: `send_list`: -1 marks an unused slot; otherwise a local leaf index of the sending device. `m2l_list`: -1 marks an offset without source; otherwise a column of the device's pool. `near_list`: -1 marks an empty entry; entry 0 is the leaf itself.
All inputs are finite; a program needn't handle non-finite values.
Results may differ from the reference program's by a relative error of at most 0.004.
Values may be sent and summed in bfloat16 or wider, within the bound.
No kernel may reach another device: no remote copies, remote signals or barrier semaphores. Data moves between devices by JAX's collectives and lax.ppermute only.
A program may use at most 128 MiB of HBM per device.

```python
import jax
import jax.numpy as jnp
from jax import lax

COEF = 121
NCOMP = 9
ATOMS = 32
NEAR = 27
NOFF = 316
HALO = 16
LET = 4
LEAF_DEV = 256
LEAVES = 65536
POOL = 1280
DEVICES = 256


def draw_send_list(key, part):
    key = jax.random.fold_in(key, 11)
    first_key, second_key = jax.random.split(key)
    leaves = jax.random.randint(first_key, (DEVICES, DEVICES, LET), 0, LEAF_DEV)
    keeper = jax.random.randint(second_key, (DEVICES, DEVICES, LET), 0, 4) > 0
    drawn = jnp.where(keeper, leaves, -1)
    return drawn.at[:, 0, 0].set(LEAF_DEV - 1).astype(jnp.int32)


def draw_m2l_list(key, part):
    key = jax.random.fold_in(key, 23)
    first_key, second_key = jax.random.split(key)
    source = jax.random.randint(first_key, (NOFF, LEAVES), 0, POOL)
    keeper = jax.random.randint(second_key, (NOFF, LEAVES), 0, 5) < 3
    drawn = jnp.where(keeper, source, -1)
    column = lax.broadcasted_iota(jnp.int32, (NOFF, LEAVES), 1)
    row_ids = lax.broadcasted_iota(jnp.int32, (NOFF, LEAVES), 0)
    forced = (row_ids == 0) & (column % LEAF_DEV == 0)
    return jnp.where(forced, POOL - 1, drawn).astype(jnp.int32)


def draw_near_list(key, part):
    key = jax.random.fold_in(key, 37)
    first_key, second_key = jax.random.split(key)
    source = jax.random.randint(first_key, (NEAR, LEAVES), 0, LEAF_DEV + 2 * HALO)
    keeper = jax.random.randint(second_key, (NEAR, LEAVES), 0, 4) > 0
    drawn = jnp.where(keeper, source, -1)
    column = lax.broadcasted_iota(jnp.int32, (NEAR, LEAVES), 1)
    row_ids = lax.broadcasted_iota(jnp.int32, (NEAR, LEAVES), 0)
    drawn = jnp.where(row_ids == 0, column % LEAF_DEV + HALO, drawn)
    forced = (row_ids == 1) & (column % LEAF_DEV == 0)
    return jnp.where(forced, LEAF_DEV + 2 * HALO - 1, drawn).astype(jnp.int32)


def plant(values, rng, low, high):
    place = [jax.random.randint(jax.random.fold_in(rng, axis), (), 0, length) for axis, length in enumerate(values.shape)]
    longest = values.shape.index(max(values.shape))
    neighbour = place[:longest] + [(place[longest] + 1) % values.shape[longest]] + place[longest + 1:]
    return values.at[tuple(place)].set(low).at[tuple(neighbour)].set(high)


def steps_of(stream_key, dims, pieces, smallest, top_value):
    level = 1.0
    for axis_at, parts in pieces:
        steps = jax.random.uniform(jax.random.fold_in(jax.random.fold_in(stream_key, 6), axis_at), (parts,), jnp.float32, smallest / len(pieces), top_value / len(pieces))
        level = level * jnp.repeat(jnp.exp(steps), dims[axis_at] // parts).reshape((-1,) + (1,) * (len(dims) - 1 - axis_at))
    return level


def bell_draw(key, extent, scale, reach, cuts=(), held_as=jnp.bfloat16):
    entries = scale * jax.random.normal(key, extent, jnp.float32)
    if cuts:
        entries = entries * steps_of(key, extent, cuts, -0.22, 0.18)
    return jnp.clip(entries, -reach, reach).astype(held_as)


def setup_inputs(seed: int = 0) -> dict:
    keys = jax.random.split(jax.random.key(seed), 11)
    return {
        "multipoles": bell_draw(keys[0], (NCOMP, ATOMS, LEAVES), 1.0, 6.0, ((2, 256),)),
        "harmonics": bell_draw(keys[1], (COEF, ATOMS, LEAVES), 1.0, 6.0, ((2, 256),)),
        "positions": jnp.clip(jax.random.uniform(keys[2], (3, ATOMS, LEAVES), jnp.float32, -3.0, 3.0) * steps_of(keys[2], (3, ATOMS, LEAVES), ((2, 256),), -0.4, 0.0), -3.0, 3.0),
        "atom_counts": plant(jax.random.randint(keys[3], (LEAVES,), ATOMS // 2, ATOMS + 1), jax.random.fold_in(keys[3], 1), ATOMS // 2, ATOMS).astype(jnp.int32),
        "source_ops": bell_draw(keys[4], (NCOMP, COEF, COEF), (NCOMP * COEF) ** -0.5, 0.1875, (), jnp.float32),
        "field_ops": bell_draw(keys[5], (NCOMP, COEF, COEF), COEF ** -0.5, 0.5, (), jnp.float32),
        "m2l_ops": bell_draw(keys[6], (NOFF, COEF, COEF), (COEF * NOFF) ** -0.5, 0.03125),
        "send_list": draw_send_list(jax.random.fold_in(keys[10], 71), 0),
        "m2l_list": draw_m2l_list(jax.random.fold_in(keys[10], 71), 0),
        "near_list": draw_near_list(jax.random.fold_in(keys[10], 71), 0),
    }


softening = 0.25

def near_field(own_src, extended, near_rows):

    def one_slot(running, slot_row):
        usable = slot_row >= 0
        picked = jnp.take(extended, jnp.clip(slot_row, 0, extended.shape[2] - 1), axis=2)
        picked = jnp.where(usable[None, None, :], picked, 0.0)
        offsets = own_src[:3, :, None, :] - picked[:3, None, :, :]
        inverse = 1.0 / jnp.sqrt(lax.optimization_barrier(jnp.sum(offsets * offsets, axis=0)) + softening)
        inverse_cube = inverse * inverse * inverse
        inverse_five = inverse_cube * inverse * inverse
        charge = picked[3][None, :, :]
        weighted = charge * inverse_cube
        steep_part = 3.0 * charge * inverse_five
        along_x, along_y, along_z = (offsets[0], offsets[1], offsets[2])
        pair_terms = jnp.stack([charge * inverse, weighted * along_x, weighted * along_y, weighted * along_z, weighted - steep_part * along_x * along_x, weighted - steep_part * along_y * along_y, -steep_part * along_x * along_y, -steep_part * along_x * along_z, -steep_part * along_y * along_z])
        return (running + lax.optimization_barrier(jnp.sum(pair_terms, axis=2)), None)
    initial = jnp.zeros((9, own_src.shape[1], own_src.shape[2]), jnp.float32)
    result, unused = lax.scan(one_slot, initial, near_rows)
    return result

def reference(multipoles, harmonics, positions, atom_counts, source_ops, field_ops, m2l_ops, send_list, m2l_list, near_list):
    slot_ids = lax.broadcasted_iota(jnp.int32, positions.shape[1:], 0)
    present = slot_ids < atom_counts[None, :]
    masked = jnp.where(present[None], multipoles, jnp.zeros_like(multipoles))
    sources = jnp.einsum('cal,kal->ckl', masked.astype(jnp.float32), harmonics.astype(jnp.float32))
    moments = jnp.einsum('ckj,ckl->jl', source_ops, sources, precision=lax.Precision.HIGHEST).astype(jnp.bfloat16)
    all_src = jnp.concatenate([positions, masked[0:1].astype(jnp.float32)], axis=0)
    padded_src = jnp.pad(all_src, ((0, 0), (0, 0), (HALO, HALO)))
    bases = (jnp.arange(DEVICES, dtype=jnp.int32) * LEAF_DEV)[:, None]

    def one_device(device):
        first = (device * LEAF_DEV).astype(jnp.int32)
        own_moments = lax.dynamic_slice_in_dim(moments, first, LEAF_DEV, 1)
        send_rows = lax.dynamic_index_in_dim(send_list, device, 1, keepdims=False)
        flat_rows = send_rows.reshape(-1)
        global_rows = (bases + jnp.clip(send_rows, 0, None)).reshape(-1).astype(jnp.int32)
        got = jnp.take(moments, global_rows, axis=1)
        got = jnp.where(flat_rows[None, :] >= 0, got, jnp.zeros_like(got))
        source_pool = jnp.concatenate([own_moments, got], axis=1)
        list_rows = lax.dynamic_slice_in_dim(m2l_list, first, LEAF_DEV, 1)
        gathered = jnp.take(source_pool, jnp.clip(list_rows, 0, source_pool.shape[1] - 1), axis=1)
        gathered = jnp.where(list_rows[None] >= 0, gathered, jnp.zeros_like(gathered))
        local_exp = jnp.einsum('kol,okj->jl', gathered.astype(jnp.float32), m2l_ops.astype(jnp.float32))
        derived = jnp.einsum('ckj,jl->ckl', field_ops, local_exp, precision=lax.Precision.HIGHEST).astype(jnp.bfloat16)
        own_harm = lax.dynamic_slice_in_dim(harmonics, first, LEAF_DEV, 2)
        far_part = jnp.einsum('ckl,kal->cal', derived.astype(jnp.float32), own_harm.astype(jnp.float32))
        own_src = lax.dynamic_slice_in_dim(all_src, first, LEAF_DEV, 2)
        extended = lax.dynamic_slice_in_dim(padded_src, first, LEAF_DEV + 2 * HALO, 2)
        near_rows = lax.dynamic_slice_in_dim(near_list, first, LEAF_DEV, 1)
        near_part = near_field(own_src, extended, near_rows)
        own_present = lax.dynamic_slice_in_dim(present, first, LEAF_DEV, 1)
        return jnp.where(own_present[None], far_part + near_part, 0.0)
    stacked = lax.map(one_device, jnp.arange(DEVICES, dtype=jnp.int32))
    return jnp.moveaxis(stacked, 0, 2).reshape(NCOMP, ATOMS, LEAVES)
```

```python
import functools

import jax
import jax.numpy as jnp
from jax import lax
from jax.experimental import pallas as pl
from jax.experimental.pallas import tpu as pltpu
from jax.sharding import PartitionSpec as P

F32 = jnp.float32
BF = jnp.bfloat16
HALO = 16
NB, LAG, M = 6, 5, 80


def padded(value, axes, width):
    count, length = (lax.axis_size(axes), value.shape[2])
    up = [(i, (i + 1) % count) for i in range(count - 1)]
    down = [(j, i) for i, j in up]
    before = lax.ppermute(value[:, :, length - width :], axes, up)
    after = lax.ppermute(value[:, :, :width], axes, down)
    return jnp.concatenate([before, value, after], axis=2)


def near_kernel(near_ref, own_ref, ext_ref, out_ref, picked, keys_s, srt, nsm):
    n_near, leaves = near_ref.shape
    atoms = 32
    blocks = ext_ref.shape[1] // 128
    for lb in range(2):
        lanes = slice(lb * 128, lb * 128 + 128)
        pos = srt[:, lanes]
        safe = jnp.maximum(pos, 0)
        lane = safe & 127
        blk = safe >> 7
        for r in range(0, 32, 8):
            cnt = None
            for k in range(blocks):
                t = jnp.take_along_axis(ext_ref[128:136, k * 128:k * 128 + 128], lane[r:r + 8], axis=1, mode="promise_in_bounds")
                cnt = t if cnt is None else jnp.where(blk[r:r + 8] == k, t, cnt)
            key = jnp.where(pos[r:r + 8] >= 0, cnt.astype(jnp.int32) * 512 + safe[r:r + 8], 0)
            keys_s[lb, r:r + 8, :] = key
    ks = [keys_s[:, r, :] for r in range(32)]
    for a, b in batcher(32):
        hi = jnp.maximum(ks[a], ks[b]); lo = jnp.minimum(ks[a], ks[b])
        ks[a], ks[b] = hi, lo
    for r in range(32):
        keys_s[:, r, :] = ks[r]
    for r in range(n_near):
        for lb in range(2):
            m = jnp.max(ks[r][lb:lb + 1].astype(F32))
            nsm[lb, r] = m.astype(jnp.int32) >> 9

    for lb in range(2):
        lanes = slice(lb * 128, lb * 128 + 128)
        def gather(n, _):
            key = keys_s[lb, pl.ds(n, 1), :]
            pos = jnp.broadcast_to(key & 511, (8, 128))
            lane = pos & 127
            blk = pos >> 7
            live = jnp.broadcast_to(key, (8, 128)) > 0
            for c in range(4):
                for r in range(0, atoms, 8):
                    v = None
                    for k in range(blocks):
                        t = jnp.take_along_axis(ext_ref[c * 32 + r:c * 32 + r + 8, k * 128:k * 128 + 128], lane, axis=1, mode="promise_in_bounds")
                        v = t if v is None else jnp.where(blk == k, t, v)
                    if c == 3:
                        v = jnp.where(live, v, 0.0)
                    picked[n, c * 32 + r:c * 32 + r + 8, :] = v
            return 0
        lax.fori_loop(0, n_near, gather, 0)
        AG = 2
        for a0 in range(0, atoms, 8 * AG):
            own = [[own_ref[c * 32 + a0 + 8 * g:c * 32 + a0 + 8 * g + 8, lanes] for c in range(3)] for g in range(AG)]
            def entry(n, carry):
                def chunk(k, carry):
                    carry = list(carry)
                    for bb in range(4):
                        b = k * 4 + bb
                        src = [picked[n, pl.ds(c * 32 + b, 1), :] for c in range(4)]
                        for g in range(AG):
                            dx = own[g][0] - src[0]
                            dy = own[g][1] - src[1]
                            dz = own[g][2] - src[2]
                            w = lax.rsqrt(dx * dx + dy * dy + (dz * dz + 0.25))
                            w2 = w * w
                            qw = src[3] * w
                            q3 = qw * w2
                            s = q3 * w2
                            sx = s * dx
                            sy = s * dy
                            acc = carry[g * 10:g * 10 + 10]
                            new = [qw, q3 * dx, q3 * dy, q3 * dz, q3, sx * dx, sy * dy, sx * dy, sx * dz, sy * dz]
                            carry[g * 10:g * 10 + 10] = [p + t for p, t in zip(acc, new)]
                    return tuple(carry)
                return lax.fori_loop(0, (nsm[lb, n] + 3) // 4, chunk, carry)
            zero = jnp.zeros((8, 128), F32)
            res = lax.fori_loop(0, n_near, entry, tuple([zero] * (10 * AG)))
            for g in range(AG):
                p, gx, gy, gz, q3, xx, yy, xy, xz, yz = res[g * 10:g * 10 + 10]
                final = [p, gx, gy, gz, q3 - 3.0 * xx, q3 - 3.0 * yy, -3.0 * xy, -3.0 * xz, -3.0 * yz]
                for c in range(9):
                    out_ref[c, a0 + 8 * g:a0 + 8 * g + 8, lanes] = final[c]

def batcher(n):
    out = []
    p = 1
    while p < n:
        k = p
        while k >= 1:
            for j in range(k % p, n - k, 2 * k):
                for i in range(min(k, n - j - k)):
                    if (i + j) // (2 * p) == (i + j + k) // (2 * p):
                        out.append((i + j, i + j + k))
            k //= 2
        p *= 2
    return out

def near(near_rows, own, ext):
    V=pltpu.VMEM
    srt = jnp.pad(near_rows, ((0, 32 - near_rows.shape[0]), (0, 0)), constant_values=-1)
    e = jnp.pad(ext, ((0,0),(0,0),(0, 384 - ext.shape[2]))).reshape(160, 384)
    def kern(near_ref, srt, own_ref, ext_ref, out_ref, picked, keys_s, nsm):
        near_kernel(near_ref, own_ref, ext_ref, out_ref, picked, keys_s, srt, nsm)
    return pl.pallas_call(kern, out_shape=jax.ShapeDtypeStruct((9, 32, 256), F32),
        in_specs=[pl.BlockSpec(memory_space=V)]*4, out_specs=pl.BlockSpec(memory_space=V),
        scratch_shapes=[V((27, 128, 128), F32), V((2, 32, 128), jnp.int32), pltpu.SMEM((2, 32), jnp.int32)],
        compiler_params=pltpu.CompilerParams(vmem_limit_bytes=24*1024*1024))(near_rows, srt, own.reshape(96, 256), e)

def m2l_inner(idx_ref, ops_ref, own_ref, inc_ref, out_ref, idx_s, pool, ptmp, xs, t_s, g_s, acc, *ra):
    n_off, leaves = idx_ref.shape
    coef = ops_ref.shape[0]
    n_pad = idx_s.shape[0]
    full = n_off // 16
    ra = [ra[:NB], ra[NB:]]
    idx_s[...] = jnp.full_like(idx_s, -1)
    idx_s[0:n_off, :] = idx_ref[...]
    ptmp[...] = jnp.zeros_like(ptmp)
    for h in range(5):
        if h == 0:
            ptmp[0:coef, :] = own_ref[...].astype(F32)
        else:
            ptmp[0:coef, :] = inc_ref[(h - 1) * 256:h * 256, :].astype(F32).T
        for c in range(8):
            pool[c, h * 16:(h + 1) * 16, :] = ptmp[c * 16:(c + 1) * 16, :].astype(BF)
    t_s[...] = jnp.zeros_like(t_s)
    g_s[...] = jnp.zeros_like(g_s)
    acc[...] = jnp.zeros_like(acc)
    xs[...] = jnp.zeros_like(xs)
    xs[0:coef * 16, 0:coef] = ops_ref[:, 0:16, :].astype(F32).reshape(coef * 16, coef)
    tail = n_off - full * 16
    for k in range(coef):
        xs[4096 + k * 16:4096 + k * 16 + tail, 0:coef] = ops_ref[k, full * 16:n_off, :].astype(F32)
    iota = lax.broadcasted_iota(jnp.int32, (256, 256), 0).astype(F32).astype(BF)
    one = jnp.ones((256, 256), BF)
    zero = jnp.zeros((256, 256), BF)
    half = coef - 64

    def hot(o):
        row = idx_s[pl.ds(o, 1), :]
        lo = jnp.where(row >= 0, row & 255, -1).astype(F32).astype(BF)
        return jnp.where(iota == lo, one, zero)

    def relayout(b):
        c = jnp.minimum(b // 2 + 1, full - 1)
        k0 = lax.rem(b, 2) * half
        xs[pl.ds(pl.multiple_of(lax.rem(b // 2 + 1, 2) * 2048 + k0 * 16, 16), 1024), 0:coef] = ops_ref[pl.ds(k0, 64), pl.ds(pl.multiple_of(c * 16, 16), 16), :].astype(F32).reshape(1024, coef)

    def take_ops(b, w):
        c = b // 2
        slot = jnp.where(c == full, 2, lax.rem(c, 2))
        o8 = lax.rem(b, 2) * 8
        for m in range(2):
            for u in range(2):
                x = xs[pl.ds(slot * 2048 + o8 + 4 * w + 2 * m + u, 128, stride=16), :]
                t_s[w, m, 0:128, 128 * u:128 * u + 128] = x.astype(BF).T

    def pop_dot1(m, slot, u, c, o, buf):
        r = pltpu.matmul_pop(buf)
        hi = idx_s[pl.ds(o, 1), :] >> 8
        g = r[0:16]
        for h in range(1, 5):
            g = jnp.where(hi == h, r[16 * h:16 * h + 16], g)
        g_s[slot, m, u * 128 + c * 16:u * 128 + (c + 1) * 16, :] = g.astype(BF)

    def pop_dot2(m, part, buf):
        acc[m, part * M:(part + 1) * M, :] += pltpu.matmul_pop(buf)

    seq = [("a", 0, c) for c in range(8)] + [("d", 0, 0), ("d", 0, 1)] + [("a", 1, c) for c in range(8)]

    def pop(m, w, item, base, buf):
        kind, u, c = item
        if kind == "a":
            pop_dot1(m, w, u, c, base + 2 * m + u, buf)
        else:
            pop_dot2(m, c, buf)

    def issue(b, w, s, base, last=False):
        kind, u, c = seq[s]
        for m in range(2):
            buf = ra[m][s % NB]
            if kind == "a":
                pltpu.matmul_acc_lhs(buf, pool[c], load_staged_rhs=0 if c == 0 else None)
            else:
                pltpu.matmul_acc_lhs(buf, t_s[1 - w, m, c * M:(c + 1) * M, :], load_staged_rhs=1 if c == 0 else None)

    n_body = n_pad // 8
    for m in range(2):
        pltpu.matmul_push_rhs(hot(2 * m), 0, m)
    for m in range(2):
        pltpu.matmul_push_rhs(zero, 1, m)
        for s in range(len(seq) - LAG, len(seq)):
            pltpu.matmul_acc_lhs(ra[m][s % NB], pool[0], load_staged_rhs=1 if s == len(seq) - LAG else None)

    def body(b, _):
        for w in range(2):
            base = b * 8 + 4 * w
            prev = jnp.maximum(base - 4, 0)
            for s in range(len(seq)):
                issue(b, w, s, base)
                if s == 0:
                    for m in range(2):
                        pltpu.matmul_push_rhs(hot(base + 2 * m + 1), 0, m)
                if s == LAG:
                    for m in range(2):
                        pltpu.matmul_push_rhs(g_s[1 - w, m], 1, m)
                if s == 10:
                    for m in range(2):
                        pltpu.matmul_push_rhs(hot(jnp.minimum(base + 4 + 2 * m, n_pad - 1)), 0, m)
                p = s - LAG
                for m in range(2):
                    if p >= 0:
                        pop(m, w, seq[p], base, ra[m][p % NB])
                    else:
                        pop(m, 1 - w, seq[p + len(seq)], prev, ra[m][(p + len(seq)) % NB])
                if s == 11:
                    take_ops(b, w)
        relayout(b)
        return 0

    lax.fori_loop(0, n_body, body, 0)
    nb = len(seq)
    for s in range(nb - LAG, nb):
        for m in range(2):
            pop(m, 1, seq[s], n_pad - 4, ra[m][s % NB])
    for m in range(2):
        pltpu.matmul_acc_lhs(ra[m][0], pool[0], load_staged_rhs=0)
    junk = [pltpu.matmul_pop(ra[m][0]) for m in range(2)]
    for m in range(2):
        pltpu.matmul_push_rhs(g_s[1, m], 1, m)
        for c in range(2):
            pltpu.matmul_acc_lhs(ra[m][c], t_s[1, m, c * M:(c + 1) * M, :], load_staged_rhs=1 if c == 0 else None)
    for m in range(2):
        for c in range(2):
            pop_dot2(m, c, ra[m][c])
    out_ref[...] = acc[0, 0:coef, :] + acc[1, 0:coef, :]

def m2l_kernel(*refs):
    accs = [pltpu.ACC(m)((M, 256), F32) for m in range(2) for _ in range(NB)]
    pl.run_scoped(functools.partial(m2l_inner, *refs), *accs)

def m2l(idx, ops, own, inc):
    n_off = idx.shape[0]
    coef = ops.shape[0]
    n_pad = -(-n_off // 8) * 8
    V = pltpu.VMEM
    return pl.pallas_call(
        m2l_kernel,
        out_shape=jax.ShapeDtypeStruct((coef, 256), F32),
        in_specs=[pl.BlockSpec(memory_space=V)] * 4,
        out_specs=pl.BlockSpec(memory_space=V),
        scratch_shapes=[V((n_pad, 256), jnp.int32), V((8, M, 256), BF), V((128, 256), F32), V((3 * 2048, 128), F32),
                        V((2, 2, 2 * M, 256), BF), V((2, 2, 256, 256), BF), V((2, 2 * M, 256), F32)],
        compiler_params=pltpu.CompilerParams(vmem_limit_bytes=40*1024*1024),
    )(idx, ops, own, inc)


def shards(
    multipoles,
    harmonics,
    positions,
    atom_counts,
    source_ops,
    field_ops,
    m2l_ops,
    send_list,
    m2l_list,
    near_list,
):
    axes = ("grp", "dev")
    atoms, leaves = positions.shape[1:]
    slot_ids = lax.broadcasted_iota(jnp.int32, (atoms, leaves), 0)
    present = slot_ids < atom_counts[None, :]
    masked = jnp.where(present[None], multipoles, jnp.zeros_like(multipoles))
    counts = jnp.broadcast_to(atom_counts.astype(F32)[None, None, :], (1, atoms, leaves))
    own_src = jnp.concatenate([positions, masked[0:1].astype(F32), counts], axis=0)
    extended = padded(own_src, axes, HALO)
    sources = jnp.einsum("cal,kal->ckl", masked, harmonics, preferred_element_type=F32)
    moments = jnp.einsum("ckj,ckl->jl", source_ops, sources, precision=lax.Precision.HIGHEST).astype(BF)
    coef_count = moments.shape[0]
    send_rows = send_list[0]
    slot_count = send_rows.shape[1]
    peer_count = lax.axis_size(axes)
    flat_rows = send_rows.reshape(-1)
    outgoing = jnp.take(moments, jnp.clip(flat_rows, 0, None), axis=1)
    outgoing = jnp.where(flat_rows[None, :] >= 0, outgoing, jnp.zeros_like(outgoing))
    outgoing = outgoing.T.reshape(peer_count, slot_count, coef_count)
    groups = lax.axis_size("grp")
    sectioned = outgoing.reshape(groups, peer_count // groups, slot_count, coef_count)
    arrived = lax.all_to_all(
        lax.all_to_all(sectioned, "grp", split_axis=0, concat_axis=0, tiled=True),
        "dev",
        split_axis=1,
        concat_axis=1,
        tiled=True,
    )
    incoming = arrived.reshape(peer_count * slot_count, coef_count)
    near_part = near(near_list, positions, extended)
    local_exp = m2l(m2l_list, m2l_ops.transpose(1, 0, 2), moments, incoming)
    derived = jnp.einsum("ckj,jl->ckl", field_ops, local_exp, precision=lax.Precision.HIGHEST).astype(BF)
    far_part = jnp.einsum("ckl,kal->cal", derived, harmonics, preferred_element_type=F32)
    return jnp.where(present[None], far_part + near_part, 0.0)


def solution(mesh):
    placed = (
        P(None, None, ("grp", "dev")),
        P(None, None, ("grp", "dev")),
        P(None, None, ("grp", "dev")),
        P(("grp", "dev")),
        P(),
        P(),
        P(),
        P(("grp", "dev"), None, None),
        P(None, ("grp", "dev")),
        P(None, ("grp", "dev")),
    )
    inner = jax.shard_map(
        shards, mesh=mesh, in_specs=placed, out_specs=P(None, None, ("grp", "dev")), check_vma=False
    )

    def whole(*args):
        with jax.sharding.use_abstract_mesh(mesh.abstract_mesh):
            return inner(*args)

    return whole
```

```python
import functools

import jax
import jax.numpy as jnp
from jax import lax
from jax.experimental import pallas as pl
from jax.experimental.pallas import tpu as pltpu
from jax.sharding import PartitionSpec as P

F32 = jnp.float32
BF = jnp.bfloat16
HALO = 16
def padded(value, axes, width):
    count, length = (lax.axis_size(axes), value.shape[2])
    up = [(i, (i + 1) % count) for i in range(count - 1)]
    down = [(j, i) for i, j in up]
    before = lax.ppermute(value[:, :, length - width :], axes, up)
    after = lax.ppermute(value[:, :, :width], axes, down)
    return jnp.concatenate([before, value, after], axis=2)


NB, LAG, M = 6, 5, 80
STEP = 4


def batcher(n):
    out = []
    p = 1
    while p < n:
        k = p
        while k >= 1:
            for j in range(k % p, n - k, 2 * k):
                for i in range(min(k, n - j - k)):
                    if (i + j) // (2 * p) == (i + j + k) // (2 * p):
                        out.append((i + j, i + j + k))
            k //= 2
        p *= 2
    return out


def take_lanes(ref, row, lane, blk, blocks):
    value = None
    for k in range(blocks):
        t = jnp.take_along_axis(
            ref[row : row + 8, k * 128 : k * 128 + 128], lane, axis=1, mode="promise_in_bounds"
        )
        value = t if value is None else jnp.where(blk == k, t, value)
    return value


def near_setup(near_ref, own_ref, ext_ref, keys_s, picked, own_s, nacc, cnt_s):
    blocks = ext_ref.shape[1] // 128
    n_near = picked.shape[1] - 1
    nacc[...] = jnp.zeros_like(nacc)
    for lb in range(2):
        lanes = slice(lb * 128, lb * 128 + 128)
        own_s[lb] = own_ref[:, lanes]
        picked[lb, n_near] = jnp.zeros((128, 128), F32)
        for r in range(0, 32, 8):
            pos = near_ref[r : r + 8, lanes]
            safe = jnp.maximum(pos, 0)
            count = take_lanes(ext_ref, 128, safe & 127, safe >> 7, blocks)
            keys_s[lb, r : r + 8, :] = jnp.where(pos >= 0, count.astype(jnp.int32) * 512 + safe, 0)
    ks = [keys_s[:, r, :] for r in range(32)]
    for a, b in batcher(32):
        ks[a], ks[b] = jnp.maximum(ks[a], ks[b]), jnp.minimum(ks[a], ks[b])
    total = jnp.int32(0)
    for r in range(32):
        keys_s[:, r, :] = ks[r]
    for r in range(n_near):
        for lb in range(2):
            top = jnp.max(ks[r][lb : lb + 1].astype(F32)).astype(jnp.int32) >> 9
            chunks = (top + STEP - 1) // STEP
            cnt_s[lb, r] = chunks
            total += chunks
    for lb in range(2):
        cnt_s[lb, n_near] = 0

    def gather(n, _):
        for lb in range(2):
            key = jnp.broadcast_to(keys_s[lb, pl.ds(n, 1), :], (8, 128))
            pos = key & 511
            for c in range(4):
                for r in range(0, 32, 8):
                    v = take_lanes(ext_ref, c * 32 + r, pos & 127, pos >> 7, blocks)
                    if c == 3:
                        v = jnp.where(key > 0, v, 0.0)
                    picked[lb, n, c * 32 + r : c * 32 + r + 8, :] = v
        return 0

    lax.fori_loop(0, n_near, gather, 0)
    return total


def near_item(state, picked, own_s, nacc, cnt_s):
    lb, n, k = state
    n_near = picked.shape[1] - 1
    for g in range(4):
        own = [own_s[lb, c * 32 + 8 * g : c * 32 + 8 * g + 8, :] for c in range(3)]
        acc = [nacc[lb, g, i] for i in range(10)]
        for bb in range(STEP):
            src = [picked[lb, n, pl.ds(c * 32 + k * STEP + bb, 1), :] for c in range(4)]
            dx = own[0] - src[0]
            dy = own[1] - src[1]
            dz = own[2] - src[2]
            w = lax.rsqrt(dx * dx + dy * dy + (dz * dz + 0.25))
            w2 = w * w
            qw = src[3] * w
            q3 = qw * w2
            s = q3 * w2
            sx = s * dx
            sy = s * dy
            new = [qw, q3 * dx, q3 * dy, q3 * dz, q3, sx * dx, sy * dy, sx * dy, sx * dz, sy * dz]
            acc = [p + t for p, t in zip(acc, new)]
        for i in range(10):
            nacc[lb, g, i] = acc[i]
    k1 = k + 1
    over = k1 >= cnt_s[lb, n]
    n1 = jnp.where(over, n + 1, n)
    k1 = jnp.where(over, 0, k1)
    out = cnt_s[lb, jnp.minimum(n1, n_near)] == 0
    done = out & (lb == 1)
    lb1 = jnp.where(out, 1, lb)
    n1 = jnp.where(out, jnp.where(done, n_near, 0), n1)
    n1 = jnp.where(cnt_s[lb1, n1] == 0, n_near, n1)
    return lb1, n1, k1


def near_first(cnt_s, n_near):
    lb = jnp.where(cnt_s[0, 0] == 0, 1, 0)
    return lb, jnp.where(cnt_s[lb, 0] == 0, n_near, 0), jnp.int32(0)


def near_finish(near_out, nacc):
    for lb in range(2):
        for g in range(4):
            p, gx, gy, gz, q3, xx, yy, xy, xz, yz = [nacc[lb, g, i] for i in range(10)]
            final = [p, gx, gy, gz, q3 - 3.0 * xx, q3 - 3.0 * yy, -3.0 * xy, -3.0 * xz, -3.0 * yz]
            for c in range(9):
                near_out[c, 8 * g : 8 * g + 8, lb * 128 : lb * 128 + 128] = final[c]


def near_kernel(near_ref, pos_ref, ext_ref, near_out, keys_s, picked, own_s, nacc, cnt_s):
    n_near = picked.shape[1] - 1
    total = near_setup(near_ref, pos_ref, ext_ref, keys_s, picked, own_s, nacc, cnt_s)
    first = near_first(cnt_s, n_near)
    lax.fori_loop(0, total, lambda _, st: near_item(st, picked, own_s, nacc, cnt_s), first)
    near_finish(near_out, nacc)


def near(near_rows, pos, ext):
    n_near = near_rows.shape[0]
    near_pad = jnp.pad(near_rows, ((0, 32 - n_near), (0, 0)), constant_values=-1)
    ext_pad = jnp.pad(ext, ((0, 0), (0, 0), (0, -ext.shape[2] % 128))).reshape(5 * 32, -1)
    V = pltpu.VMEM
    vm = pl.BlockSpec(memory_space=V)
    return pl.pallas_call(
        near_kernel,
        out_shape=jax.ShapeDtypeStruct((9, 32, 256), F32),
        in_specs=[vm, vm, vm],
        out_specs=vm,
        scratch_shapes=[
            V((2, 32, 128), jnp.int32),
            V((2, n_near + 1, 128, 128), F32),
            V((2, 96, 128), F32),
            V((2, 4, 10, 8, 128), F32),
            pltpu.SMEM((2, n_near + 1), jnp.int32),
        ],
        compiler_params=pltpu.CompilerParams(vmem_limit_bytes=12 * 1024 * 1024),
        cost_estimate=pl.CostEstimate(flops=250_000_000, bytes_accessed=40_000_000, transcendentals=7_000_000),
    )(near_pad, pos.reshape(96, 256), ext_pad)


def fields_inner(
    idx_ref, ops_ref, own_ref, inc_ref, out_ref, idx_s, pool, ptmp, xs, t_s, g_s, acc, *ra
):
    n_off, leaves = idx_ref.shape
    coef = ops_ref.shape[0]
    n_pad = idx_s.shape[0]
    full = n_off // 16
    ra = [ra[:NB], ra[NB:]]
    idx_s[...] = jnp.full_like(idx_s, -1)
    idx_s[0:n_off, :] = idx_ref[...]
    ptmp[...] = jnp.zeros_like(ptmp)
    for h in range(5):
        if h == 0:
            ptmp[0:coef, :] = own_ref[...].astype(F32)
        else:
            ptmp[0:coef, :] = inc_ref[(h - 1) * 256 : h * 256, :].astype(F32).T
        for c in range(8):
            pool[c, h * 16 : (h + 1) * 16, :] = ptmp[c * 16 : (c + 1) * 16, :].astype(BF)
    t_s[...] = jnp.zeros_like(t_s)
    g_s[...] = jnp.zeros_like(g_s)
    acc[...] = jnp.zeros_like(acc)
    xs[...] = jnp.zeros_like(xs)
    xs[0 : coef * 16, 0:coef] = ops_ref[:, 0:16, :].astype(F32).reshape(coef * 16, coef)
    tail = n_off - full * 16
    for k in range(coef):
        xs[4096 + k * 16 : 4096 + k * 16 + tail, 0:coef] = ops_ref[k, full * 16 : n_off, :].astype(F32)
    iota = lax.broadcasted_iota(jnp.int32, (256, 256), 0).astype(F32).astype(BF)
    one = jnp.ones((256, 256), BF)
    zero = jnp.zeros((256, 256), BF)
    half = coef - 64

    def hot(o):
        row = idx_s[pl.ds(o, 1), :]
        lo = jnp.where(row >= 0, row & 255, -1).astype(F32).astype(BF)
        return jnp.where(iota == lo, one, zero)

    def relayout(b):
        c = jnp.minimum(b // 2 + 1, full - 1)
        k0 = lax.rem(b, 2) * half
        to = pl.multiple_of(lax.rem(b // 2 + 1, 2) * 2048 + k0 * 16, 16)
        part = ops_ref[pl.ds(k0, 64), pl.ds(pl.multiple_of(c * 16, 16), 16), :]
        xs[pl.ds(to, 1024), 0:coef] = part.astype(F32).reshape(1024, coef)

    def take_ops(b, w):
        c = b // 2
        slot = jnp.where(c == full, 2, lax.rem(c, 2))
        o8 = lax.rem(b, 2) * 8
        for m in range(2):
            for u in range(2):
                x = xs[pl.ds(slot * 2048 + o8 + 4 * w + 2 * m + u, 128, stride=16), :]
                t_s[w, m, 0:128, 128 * u : 128 * u + 128] = x.astype(BF).T

    def pop_dot1(m, slot, u, c, o, buf):
        r = pltpu.matmul_pop(buf)
        hi = idx_s[pl.ds(o, 1), :] >> 8
        g = r[0:16]
        for h in range(1, 5):
            g = jnp.where(hi == h, r[16 * h : 16 * h + 16], g)
        g_s[slot, m, u * 128 + c * 16 : u * 128 + (c + 1) * 16, :] = g.astype(BF)

    def pop_dot2(m, part, buf):
        acc[m, part * M : (part + 1) * M, :] += pltpu.matmul_pop(buf)

    seq = [("a", 0, c) for c in range(8)] + [("d", 0, 0), ("d", 0, 1)] + [("a", 1, c) for c in range(8)]

    def pop(m, w, item, base, buf):
        kind, u, c = item
        if kind == "a":
            pop_dot1(m, w, u, c, base + 2 * m + u, buf)
        else:
            pop_dot2(m, c, buf)

    def issue(w, s):
        kind, u, c = seq[s]
        for m in range(2):
            buf = ra[m][s % NB]
            if kind == "a":
                pltpu.matmul_acc_lhs(buf, pool[c], load_staged_rhs=0 if c == 0 else None)
            else:
                pltpu.matmul_acc_lhs(buf, t_s[1 - w, m, c * M : (c + 1) * M, :], load_staged_rhs=1 if c == 0 else None)

    n_body = n_pad // 8
    for m in range(2):
        pltpu.matmul_push_rhs(hot(2 * m), 0, m)
    for m in range(2):
        pltpu.matmul_push_rhs(zero, 1, m)
        for s in range(len(seq) - LAG, len(seq)):
            pltpu.matmul_acc_lhs(ra[m][s % NB], pool[0], load_staged_rhs=1 if s == len(seq) - LAG else None)

    def body(b, _):
        for w in range(2):
            base = b * 8 + 4 * w
            prev = jnp.maximum(base - 4, 0)
            for s in range(len(seq)):
                issue(w, s)
                if s == 0:
                    for m in range(2):
                        pltpu.matmul_push_rhs(hot(base + 2 * m + 1), 0, m)
                if s == LAG:
                    for m in range(2):
                        pltpu.matmul_push_rhs(g_s[1 - w, m], 1, m)
                if s == 10:
                    for m in range(2):
                        pltpu.matmul_push_rhs(hot(jnp.minimum(base + 4 + 2 * m, n_pad - 1)), 0, m)
                p = s - LAG
                for m in range(2):
                    if p >= 0:
                        pop(m, w, seq[p], base, ra[m][p % NB])
                    else:
                        pop(m, 1 - w, seq[p + len(seq)], prev, ra[m][(p + len(seq)) % NB])
                if s == 11:
                    take_ops(b, w)
        relayout(b)
        return 0

    lax.fori_loop(0, n_body, body, 0)
    for s in range(len(seq) - LAG, len(seq)):
        for m in range(2):
            pop(m, 1, seq[s], n_pad - 4, ra[m][s % NB])
    for m in range(2):
        pltpu.matmul_acc_lhs(ra[m][0], pool[0], load_staged_rhs=0)
    for m in range(2):
        pltpu.matmul_pop(ra[m][0])
    for m in range(2):
        pltpu.matmul_push_rhs(g_s[1, m], 1, m)
        for c in range(2):
            pltpu.matmul_acc_lhs(ra[m][c], t_s[1, m, c * M : (c + 1) * M, :], load_staged_rhs=1 if c == 0 else None)
    for m in range(2):
        for c in range(2):
            pop_dot2(m, c, ra[m][c])
    out_ref[...] = acc[0, 0:coef, :] + acc[1, 0:coef, :]


def m2l_kernel(*refs):
    accs = [pltpu.ACC(m)((M, 256), F32) for m in range(2) for _ in range(NB)]
    pl.run_scoped(functools.partial(fields_inner, *refs), *accs)


def far_kernel(local_ref, near_ref, field_ref, harm_ref, count_ref, out_ref, der):
    coef = local_ref.shape[0]
    local = local_ref[...]
    for c in range(9):
        d = jnp.dot(field_ref[c], local, precision=lax.Precision.HIGHEST, preferred_element_type=F32)
        d = d.astype(BF).astype(F32)
        for lb in range(2):
            der[lb, c * 128 : c * 128 + coef, :] = d[:, lb * 128 : lb * 128 + 128]
    for lb in range(2):
        lanes = slice(lb * 128, lb * 128 + 128)
        for a0 in range(0, 32, 16):
            start = tuple(near_ref[c, a0 + 8 * g : a0 + 8 * g + 8, lanes] for c in range(9) for g in range(2))

            def add(i, sums):
                sums = list(sums)
                for u in range(11):
                    k = i * 11 + u
                    h = harm_ref[k, a0 : a0 + 16, lanes].astype(F32)
                    for c in range(9):
                        d = der[lb, pl.ds(c * 128 + k, 1), :]
                        for g in range(2):
                            sums[2 * c + g] = sums[2 * c + g] + d * h[8 * g : 8 * g + 8]
                return tuple(sums)

            sums = lax.fori_loop(0, coef // 11, add, start)
            for g in range(2):
                atom = lax.broadcasted_iota(jnp.int32, (8, 128), 0) + (a0 + 8 * g)
                present = atom < count_ref[0:1, lanes]
                for c in range(9):
                    out_ref[c, a0 + 8 * g : a0 + 8 * g + 8, lanes] = jnp.where(present, sums[2 * c + g], 0.0)


def fields_of(idx, ops, own, inc, near_part, field_ops, harmonics, counts):
    n_off = idx.shape[0]
    coef = ops.shape[0]
    n_pad = -(-n_off // 8) * 8
    V = pltpu.VMEM
    vm = pl.BlockSpec(memory_space=V)
    local = pl.pallas_call(
        m2l_kernel,
        out_shape=jax.ShapeDtypeStruct((coef, 256), F32),
        in_specs=[vm] * 4,
        out_specs=vm,
        scratch_shapes=[
            V((n_pad, 256), jnp.int32),
            V((8, M, 256), BF),
            V((128, 256), F32),
            V((3 * 2048, 128), F32),
            V((2, 2, 2 * M, 256), BF),
            V((2, 2, 256, 256), BF),
            V((2, 2 * M, 256), F32),
        ],
        compiler_params=pltpu.CompilerParams(vmem_limit_bytes=24 * 1024 * 1024),
        cost_estimate=pl.CostEstimate(flops=30_000_000_000, bytes_accessed=12_000_000, transcendentals=0),
    )(idx, ops, own, inc)
    return pl.pallas_call(
        far_kernel,
        out_shape=jax.ShapeDtypeStruct((9, 32, 256), F32),
        in_specs=[vm] * 5,
        out_specs=vm,
        scratch_shapes=[V((2, 9 * 128, 128), F32)],
        compiler_params=pltpu.CompilerParams(vmem_limit_bytes=24 * 1024 * 1024),
        cost_estimate=pl.CostEstimate(flops=500_000_000, bytes_accessed=5_000_000, transcendentals=0),
    )(local, near_part, field_ops, harmonics, counts)


def shards(
    multipoles,
    harmonics,
    positions,
    atom_counts,
    source_ops,
    field_ops,
    m2l_ops,
    send_list,
    m2l_list,
    near_list,
):
    axes = ("grp", "dev")
    atoms, leaves = positions.shape[1:]
    slot_ids = lax.broadcasted_iota(jnp.int32, (atoms, leaves), 0)
    present = slot_ids < atom_counts[None, :]
    masked = jnp.where(present[None], multipoles, jnp.zeros_like(multipoles))
    counts = jnp.broadcast_to(atom_counts.astype(F32)[None, None, :], (1, atoms, leaves))
    own_src = jnp.concatenate([positions, masked[0:1].astype(F32), counts], axis=0)
    extended = padded(own_src, axes, HALO)
    sources = jnp.einsum("cal,kal->ckl", masked, harmonics, preferred_element_type=F32)
    moments = jnp.einsum("ckj,ckl->jl", source_ops, sources, precision=lax.Precision.HIGHEST).astype(BF)
    coef_count = moments.shape[0]
    send_rows = send_list[0]
    slot_count = send_rows.shape[1]
    peer_count = lax.axis_size(axes)
    flat_rows = send_rows.reshape(-1)
    outgoing = jnp.take(moments, jnp.clip(flat_rows, 0, None), axis=1)
    outgoing = jnp.where(flat_rows[None, :] >= 0, outgoing, jnp.zeros_like(outgoing))
    outgoing = outgoing.T.reshape(peer_count, slot_count, coef_count)
    outgoing, extended = lax.optimization_barrier((outgoing, extended))
    arrived = lax.all_to_all(outgoing, axes, split_axis=0, concat_axis=0, tiled=True)
    incoming = arrived.reshape(peer_count * slot_count, coef_count)
    near_part = near(near_list, positions, extended)
    return fields_of(
        m2l_list, m2l_ops.transpose(1, 0, 2), moments, incoming, near_part, field_ops, harmonics, atom_counts.reshape(1, leaves)
    )


def solution(mesh):
    placed = (
        P(None, None, ("grp", "dev")),
        P(None, None, ("grp", "dev")),
        P(None, None, ("grp", "dev")),
        P(("grp", "dev")),
        P(),
        P(),
        P(),
        P(("grp", "dev"), None, None),
        P(None, ("grp", "dev")),
        P(None, ("grp", "dev")),
    )
    inner = jax.shard_map(
        shards, mesh=mesh, in_specs=placed, out_specs=P(None, None, ("grp", "dev")), check_vma=False
    )

    def whole(*args):
        with jax.sharding.use_abstract_mesh(mesh.abstract_mesh):
            return inner(*args)

    return whole
```

```python
import functools

import jax
import jax.numpy as jnp
from jax import lax
from jax.experimental import pallas as pl
from jax.experimental.pallas import tpu as pltpu
from jax.sharding import PartitionSpec as P

F32 = jnp.float32
BF = jnp.bfloat16
HALO = 16
def padded(value, axes, width):
    count, length = (lax.axis_size(axes), value.shape[2])
    up = [(i, (i + 1) % count) for i in range(count - 1)]
    down = [(j, i) for i, j in up]
    before = lax.ppermute(value[:, :, length - width :], axes, up)
    after = lax.ppermute(value[:, :, :width], axes, down)
    return jnp.concatenate([before, value, after], axis=2)


NB, LAG, M = 6, 5, 80
STEP = 4


def batcher(n):
    out = []
    p = 1
    while p < n:
        k = p
        while k >= 1:
            for j in range(k % p, n - k, 2 * k):
                for i in range(min(k, n - j - k)):
                    if (i + j) // (2 * p) == (i + j + k) // (2 * p):
                        out.append((i + j, i + j + k))
            k //= 2
        p *= 2
    return out


def take_lanes(ref, row, lane, blk, blocks):
    value = None
    for k in range(blocks):
        t = jnp.take_along_axis(
            ref[row : row + 8, k * 128 : k * 128 + 128], lane, axis=1, mode="promise_in_bounds"
        )
        value = t if value is None else jnp.where(blk == k, t, value)
    return value


def near_setup(near_ref, own_ref, ext_ref, keys_s, picked, own_s, nacc, cnt_s):
    blocks = ext_ref.shape[1] // 128
    n_near = picked.shape[1] - 1
    nacc[...] = jnp.zeros_like(nacc)
    for lb in range(2):
        lanes = slice(lb * 128, lb * 128 + 128)
        own_s[lb] = own_ref[:, lanes]
        picked[lb, n_near] = jnp.zeros((128, 128), F32)
        for r in range(0, 32, 8):
            pos = near_ref[r : r + 8, lanes]
            safe = jnp.maximum(pos, 0)
            count = take_lanes(ext_ref, 128, safe & 127, safe >> 7, blocks)
            keys_s[lb, r : r + 8, :] = jnp.where(pos >= 0, count.astype(jnp.int32) * 512 + safe, 0)
    ks = [keys_s[:, r, :] for r in range(32)]
    for a, b in batcher(32):
        ks[a], ks[b] = jnp.maximum(ks[a], ks[b]), jnp.minimum(ks[a], ks[b])
    total = jnp.int32(0)
    for r in range(32):
        keys_s[:, r, :] = ks[r]
    for r in range(n_near):
        for lb in range(2):
            top = jnp.max(ks[r][lb : lb + 1].astype(F32)).astype(jnp.int32) >> 9
            chunks = (top + STEP - 1) // STEP
            cnt_s[lb, r] = chunks
            total += chunks
    for lb in range(2):
        cnt_s[lb, n_near] = 0

    def gather(n, _):
        for lb in range(2):
            key = jnp.broadcast_to(keys_s[lb, pl.ds(n, 1), :], (8, 128))
            pos = key & 511
            for c in range(4):
                for r in range(0, 32, 8):
                    v = take_lanes(ext_ref, c * 32 + r, pos & 127, pos >> 7, blocks)
                    if c == 3:
                        v = jnp.where(key > 0, v, 0.0)
                    picked[lb, n, c * 32 + r : c * 32 + r + 8, :] = v
        return 0

    lax.fori_loop(0, n_near, gather, 0)
    return total


def near_item(state, picked, own_s, nacc, cnt_s):
    lb, n, k = state
    n_near = picked.shape[1] - 1
    for g in range(4):
        own = [own_s[lb, c * 32 + 8 * g : c * 32 + 8 * g + 8, :] for c in range(3)]
        acc = [nacc[lb, g, i] for i in range(10)]
        for bb in range(STEP):
            src = [picked[lb, n, pl.ds(c * 32 + k * STEP + bb, 1), :] for c in range(4)]
            dx = own[0] - src[0]
            dy = own[1] - src[1]
            dz = own[2] - src[2]
            w = lax.rsqrt(dx * dx + dy * dy + (dz * dz + 0.25))
            w2 = w * w
            qw = src[3] * w
            q3 = qw * w2
            s = q3 * w2
            sx = s * dx
            sy = s * dy
            new = [qw, q3 * dx, q3 * dy, q3 * dz, q3, sx * dx, sy * dy, sx * dy, sx * dz, sy * dz]
            acc = [p + t for p, t in zip(acc, new)]
        for i in range(10):
            nacc[lb, g, i] = acc[i]
    k1 = k + 1
    over = k1 >= cnt_s[lb, n]
    n1 = jnp.where(over, n + 1, n)
    k1 = jnp.where(over, 0, k1)
    out = cnt_s[lb, jnp.minimum(n1, n_near)] == 0
    done = out & (lb == 1)
    lb1 = jnp.where(out, 1, lb)
    n1 = jnp.where(out, jnp.where(done, n_near, 0), n1)
    n1 = jnp.where(cnt_s[lb1, n1] == 0, n_near, n1)
    return lb1, n1, k1


def near_first(cnt_s, n_near):
    lb = jnp.where(cnt_s[0, 0] == 0, 1, 0)
    return lb, jnp.where(cnt_s[lb, 0] == 0, n_near, 0), jnp.int32(0)


def near_finish(near_out, nacc):
    for lb in range(2):
        for g in range(4):
            p, gx, gy, gz, q3, xx, yy, xy, xz, yz = [nacc[lb, g, i] for i in range(10)]
            final = [p, gx, gy, gz, q3 - 3.0 * xx, q3 - 3.0 * yy, -3.0 * xy, -3.0 * xz, -3.0 * yz]
            for c in range(9):
                near_out[c, 8 * g : 8 * g + 8, lb * 128 : lb * 128 + 128] = final[c]


def near_kernel(near_ref, pos_ref, ext_ref, near_out, keys_s, picked, own_s, nacc, cnt_s):
    n_near = picked.shape[1] - 1
    total = near_setup(near_ref, pos_ref, ext_ref, keys_s, picked, own_s, nacc, cnt_s)
    first = near_first(cnt_s, n_near)
    lax.fori_loop(0, total, lambda _, st: near_item(st, picked, own_s, nacc, cnt_s), first)
    near_finish(near_out, nacc)


def near(near_rows, pos, ext):
    n_near = near_rows.shape[0]
    near_pad = jnp.pad(near_rows, ((0, 32 - n_near), (0, 0)), constant_values=-1)
    ext_pad = jnp.pad(ext, ((0, 0), (0, 0), (0, -ext.shape[2] % 128))).reshape(5 * 32, -1)
    V = pltpu.VMEM
    vm = pl.BlockSpec(memory_space=V)
    return pl.pallas_call(
        near_kernel,
        out_shape=jax.ShapeDtypeStruct((9, 32, 256), F32),
        in_specs=[vm, vm, vm],
        out_specs=vm,
        scratch_shapes=[
            V((2, 32, 128), jnp.int32),
            V((2, n_near + 1, 128, 128), F32),
            V((2, 96, 128), F32),
            V((2, 4, 10, 8, 128), F32),
            pltpu.SMEM((2, n_near + 1), jnp.int32),
        ],
        compiler_params=pltpu.CompilerParams(vmem_limit_bytes=12 * 1024 * 1024),
        cost_estimate=pl.CostEstimate(flops=250_000_000, bytes_accessed=40_000_000, transcendentals=7_000_000),
    )(near_pad, pos.reshape(96, 256), ext_pad)


def fields_inner(
    idx_ref, ops_ref, own_ref, inc_ref, out_ref, idx_s, pool, ptmp, xs, t_s, g_s, acc, *ra
):
    n_off, leaves = idx_ref.shape
    coef = ops_ref.shape[0]
    n_pad = idx_s.shape[0]
    full = n_off // 16
    ra = [ra[:NB], ra[NB:]]
    idx_s[...] = jnp.full_like(idx_s, -1)
    idx_s[0:n_off, :] = idx_ref[...]
    ptmp[...] = jnp.zeros_like(ptmp)
    for h in range(5):
        if h == 0:
            ptmp[0:coef, :] = own_ref[...].astype(F32)
        else:
            ptmp[0:coef, :] = inc_ref[(h - 1) * 256 : h * 256, :].astype(F32).T
        for c in range(8):
            pool[c, h * 16 : (h + 1) * 16, :] = ptmp[c * 16 : (c + 1) * 16, :].astype(BF)
    t_s[...] = jnp.zeros_like(t_s)
    g_s[...] = jnp.zeros_like(g_s)
    acc[...] = jnp.zeros_like(acc)
    xs[...] = jnp.zeros_like(xs)
    xs[0 : coef * 16, 0:coef] = ops_ref[:, 0:16, :].astype(F32).reshape(coef * 16, coef)
    tail = n_off - full * 16
    for k in range(coef):
        xs[4096 + k * 16 : 4096 + k * 16 + tail, 0:coef] = ops_ref[k, full * 16 : n_off, :].astype(F32)
    iota = lax.broadcasted_iota(jnp.int32, (256, 256), 0).astype(F32).astype(BF)
    one = jnp.ones((256, 256), BF)
    zero = jnp.zeros((256, 256), BF)
    half = coef - 64

    def hot(o):
        row = idx_s[pl.ds(o, 1), :]
        lo = jnp.where(row >= 0, row & 255, -1).astype(F32).astype(BF)
        return jnp.where(iota == lo, one, zero)

    def relayout(b):
        c = jnp.minimum(b // 2 + 1, full - 1)
        k0 = lax.rem(b, 2) * half
        to = pl.multiple_of(lax.rem(b // 2 + 1, 2) * 2048 + k0 * 16, 16)
        part = ops_ref[pl.ds(k0, 64), pl.ds(pl.multiple_of(c * 16, 16), 16), :]
        xs[pl.ds(to, 1024), 0:coef] = part.astype(F32).reshape(1024, coef)

    def take_ops(b, w):
        c = b // 2
        slot = jnp.where(c == full, 2, lax.rem(c, 2))
        o8 = lax.rem(b, 2) * 8
        for m in range(2):
            for u in range(2):
                x = xs[pl.ds(slot * 2048 + o8 + 4 * w + 2 * m + u, 128, stride=16), :]
                t_s[w, m, 0:128, 128 * u : 128 * u + 128] = x.astype(BF).T

    def pop_dot1(m, slot, u, c, o, buf):
        r = pltpu.matmul_pop(buf)
        hi = idx_s[pl.ds(o, 1), :] >> 8
        g = r[0:16]
        for h in range(1, 5):
            g = jnp.where(hi == h, r[16 * h : 16 * h + 16], g)
        g_s[slot, m, u * 128 + c * 16 : u * 128 + (c + 1) * 16, :] = g.astype(BF)

    def pop_dot2(m, part, buf):
        acc[m, part * M : (part + 1) * M, :] += pltpu.matmul_pop(buf)

    seq = [("a", 0, c) for c in range(8)] + [("d", 0, 0), ("d", 0, 1)] + [("a", 1, c) for c in range(8)]

    def pop(m, w, item, base, buf):
        kind, u, c = item
        if kind == "a":
            pop_dot1(m, w, u, c, base + 2 * m + u, buf)
        else:
            pop_dot2(m, c, buf)

    def issue(w, s):
        kind, u, c = seq[s]
        for m in range(2):
            buf = ra[m][s % NB]
            if kind == "a":
                pltpu.matmul_acc_lhs(buf, pool[c], load_staged_rhs=0 if c == 0 else None)
            else:
                pltpu.matmul_acc_lhs(buf, t_s[1 - w, m, c * M : (c + 1) * M, :], load_staged_rhs=1 if c == 0 else None)

    n_body = n_pad // 8
    for m in range(2):
        pltpu.matmul_push_rhs(hot(2 * m), 0, m)
    for m in range(2):
        pltpu.matmul_push_rhs(zero, 1, m)
        for s in range(len(seq) - LAG, len(seq)):
            pltpu.matmul_acc_lhs(ra[m][s % NB], pool[0], load_staged_rhs=1 if s == len(seq) - LAG else None)

    def body(b, _):
        for w in range(2):
            base = b * 8 + 4 * w
            prev = jnp.maximum(base - 4, 0)
            for s in range(len(seq)):
                issue(w, s)
                if s == 0:
                    for m in range(2):
                        pltpu.matmul_push_rhs(hot(base + 2 * m + 1), 0, m)
                if s == LAG:
                    for m in range(2):
                        pltpu.matmul_push_rhs(g_s[1 - w, m], 1, m)
                if s == 10:
                    for m in range(2):
                        pltpu.matmul_push_rhs(hot(jnp.minimum(base + 4 + 2 * m, n_pad - 1)), 0, m)
                p = s - LAG
                for m in range(2):
                    if p >= 0:
                        pop(m, w, seq[p], base, ra[m][p % NB])
                    else:
                        pop(m, 1 - w, seq[p + len(seq)], prev, ra[m][(p + len(seq)) % NB])
                if s == 11:
                    take_ops(b, w)
        relayout(b)
        return 0

    lax.fori_loop(0, n_body, body, 0)
    for s in range(len(seq) - LAG, len(seq)):
        for m in range(2):
            pop(m, 1, seq[s], n_pad - 4, ra[m][s % NB])
    for m in range(2):
        pltpu.matmul_acc_lhs(ra[m][0], pool[0], load_staged_rhs=0)
    for m in range(2):
        pltpu.matmul_pop(ra[m][0])
    for m in range(2):
        pltpu.matmul_push_rhs(g_s[1, m], 1, m)
        for c in range(2):
            pltpu.matmul_acc_lhs(ra[m][c], t_s[1, m, c * M : (c + 1) * M, :], load_staged_rhs=1 if c == 0 else None)
    for m in range(2):
        for c in range(2):
            pop_dot2(m, c, ra[m][c])
    out_ref[...] = acc[0, 0:coef, :] + acc[1, 0:coef, :]


def m2l_kernel(*refs):
    accs = [pltpu.ACC(m)((M, 256), F32) for m in range(2) for _ in range(NB)]
    pl.run_scoped(functools.partial(fields_inner, *refs), *accs)


def far_kernel(local_ref, near_ref, field_ref, harm_ref, count_ref, out_ref, der):
    coef = local_ref.shape[0]
    local = local_ref[...]
    for c in range(9):
        d = jnp.dot(field_ref[c], local, precision=lax.Precision.HIGHEST, preferred_element_type=F32)
        d = d.astype(BF).astype(F32)
        for lb in range(2):
            der[lb, c * 128 : c * 128 + coef, :] = d[:, lb * 128 : lb * 128 + 128]
    for lb in range(2):
        lanes = slice(lb * 128, lb * 128 + 128)
        for a0 in range(0, 32, 16):
            start = tuple(near_ref[c, a0 + 8 * g : a0 + 8 * g + 8, lanes] for c in range(9) for g in range(2))

            def add(i, sums):
                sums = list(sums)
                for u in range(11):
                    k = i * 11 + u
                    h = harm_ref[k, a0 : a0 + 16, lanes].astype(F32)
                    for c in range(9):
                        d = der[lb, pl.ds(c * 128 + k, 1), :]
                        for g in range(2):
                            sums[2 * c + g] = sums[2 * c + g] + d * h[8 * g : 8 * g + 8]
                return tuple(sums)

            sums = lax.fori_loop(0, coef // 11, add, start)
            for g in range(2):
                atom = lax.broadcasted_iota(jnp.int32, (8, 128), 0) + (a0 + 8 * g)
                present = atom < count_ref[0:1, lanes]
                for c in range(9):
                    out_ref[c, a0 + 8 * g : a0 + 8 * g + 8, lanes] = jnp.where(present, sums[2 * c + g], 0.0)


def fields_of(idx, ops, own, inc, near_part, field_ops, harmonics, counts):
    n_off = idx.shape[0]
    coef = ops.shape[0]
    n_pad = -(-n_off // 8) * 8
    V = pltpu.VMEM
    vm = pl.BlockSpec(memory_space=V)
    local = pl.pallas_call(
        m2l_kernel,
        out_shape=jax.ShapeDtypeStruct((coef, 256), F32),
        in_specs=[vm] * 4,
        out_specs=vm,
        scratch_shapes=[
            V((n_pad, 256), jnp.int32),
            V((8, M, 256), BF),
            V((128, 256), F32),
            V((3 * 2048, 128), F32),
            V((2, 2, 2 * M, 256), BF),
            V((2, 2, 256, 256), BF),
            V((2, 2 * M, 256), F32),
        ],
        compiler_params=pltpu.CompilerParams(vmem_limit_bytes=24 * 1024 * 1024),
        cost_estimate=pl.CostEstimate(flops=30_000_000_000, bytes_accessed=12_000_000, transcendentals=0),
    )(idx, ops, own, inc)
    return pl.pallas_call(
        far_kernel,
        out_shape=jax.ShapeDtypeStruct((9, 32, 256), F32),
        in_specs=[vm] * 5,
        out_specs=vm,
        scratch_shapes=[V((2, 9 * 128, 128), F32)],
        compiler_params=pltpu.CompilerParams(vmem_limit_bytes=24 * 1024 * 1024),
        cost_estimate=pl.CostEstimate(flops=500_000_000, bytes_accessed=5_000_000, transcendentals=0),
    )(local, near_part, field_ops, harmonics, counts)


def moments_kernel(mult_ref, harm_ref, count_ref, ops_ref, send_ref, mom_ref, out_ref, src, rows_s):
    comps, atoms, _ = mult_ref.shape
    coef = harm_ref.shape[0]
    src[...] = jnp.zeros_like(src)
    for lb in range(2):
        lanes = slice(lb * 128, lb * 128 + 128)
        held = []
        for c in range(comps):
            for g in range(atoms // 16):
                atom = lax.broadcasted_iota(jnp.int32, (16, 128), 0) + 16 * g
                value = mult_ref[c, 16 * g : 16 * g + 16, lanes].astype(F32)
                held.append(jnp.where(atom < count_ref[0:1, lanes], value, 0.0))

        def add(i, held):
            for u in range(11):
                k = i * 11 + u
                h = harm_ref[k, :, lanes].astype(F32)
                for c in range(comps):
                    part = held[2 * c] * h[0:16] + held[2 * c + 1] * h[16:32]
                    src[lb, pl.ds(c * 128 + k, 1), :] = jnp.sum(part[0:8] + part[8:16], axis=0, keepdims=True)
            return held

        lax.fori_loop(0, coef // 11, add, tuple(held))
    mom = jnp.zeros((coef, 256), F32)
    for c in range(comps):
        s = jnp.concatenate([src[lb, c * 128 : c * 128 + coef, :] for lb in range(2)], axis=1)
        mom += lax.dot_general(
            ops_ref[c], s, (((0,), (0,)), ((), ())), precision=lax.Precision.HIGHEST, preferred_element_type=F32
        )
    mom = mom.astype(BF)
    mom_ref[...] = mom
    leaf = lax.broadcasted_iota(jnp.int32, (256, 256), 0)
    slots = send_ref.shape[0]
    rows_s[...] = jnp.zeros_like(rows_s)
    for i in range(slots):
        hot = jnp.where(leaf == send_ref[i : i + 1, :], 1.0, 0.0).astype(BF)
        picked = jnp.dot(mom, hot, preferred_element_type=F32)
        rows_s[pl.ds(i, 256, stride=slots), 0:128] = jnp.pad(picked, ((0, 128 - coef), (0, 0))).T
    out_ref[...] = rows_s[:, 0:coef].astype(BF)


def moments_of(multipoles, harmonics, counts, source_ops, send_rows):
    coef = harmonics.shape[0]
    V = pltpu.VMEM
    vm = pl.BlockSpec(memory_space=V)
    peers = send_rows.shape[1] * send_rows.shape[0]
    return pl.pallas_call(
        moments_kernel,
        out_shape=(jax.ShapeDtypeStruct((coef, 256), BF), jax.ShapeDtypeStruct((peers, coef), BF)),
        in_specs=[vm] * 5,
        out_specs=(vm, vm),
        scratch_shapes=[V((2, 9 * 128, 128), F32), V((peers, 128), F32)],
        compiler_params=pltpu.CompilerParams(vmem_limit_bytes=16 * 1024 * 1024),
        cost_estimate=pl.CostEstimate(flops=500_000_000, bytes_accessed=5_000_000, transcendentals=0),
    )(multipoles, harmonics, counts, source_ops, send_rows)


def shards(
    multipoles,
    harmonics,
    positions,
    atom_counts,
    source_ops,
    field_ops,
    m2l_ops,
    send_list,
    m2l_list,
    near_list,
):
    axes = ("grp", "dev")
    atoms, leaves = positions.shape[1:]
    slot_ids = lax.broadcasted_iota(jnp.int32, (atoms, leaves), 0)
    present = slot_ids < atom_counts[None, :]
    masked = jnp.where(present[None], multipoles, jnp.zeros_like(multipoles))
    counts = jnp.broadcast_to(atom_counts.astype(F32)[None, None, :], (1, atoms, leaves))
    own_src = jnp.concatenate([positions, masked[0:1].astype(F32), counts], axis=0)
    extended = padded(own_src, axes, HALO)
    counts_row = atom_counts.reshape(1, leaves)
    moments, outgoing = moments_of(multipoles, harmonics, counts_row, source_ops, send_list[0].T)
    peer_count, slot_count = send_list.shape[1:]
    coef_count = moments.shape[0]
    outgoing = outgoing.reshape(peer_count, slot_count, coef_count)
    outgoing, extended = lax.optimization_barrier((outgoing, extended))
    arrived = lax.all_to_all(outgoing, axes, split_axis=0, concat_axis=0, tiled=True)
    incoming = arrived.reshape(peer_count * slot_count, coef_count)
    near_part = near(near_list, positions, extended)
    return fields_of(
        m2l_list, m2l_ops.transpose(1, 0, 2), moments, incoming, near_part, field_ops, harmonics, counts_row
    )


def solution(mesh):
    placed = (
        P(None, None, ("grp", "dev")),
        P(None, None, ("grp", "dev")),
        P(None, None, ("grp", "dev")),
        P(("grp", "dev")),
        P(),
        P(),
        P(),
        P(("grp", "dev"), None, None),
        P(None, ("grp", "dev")),
        P(None, ("grp", "dev")),
    )
    inner = jax.shard_map(
        shards, mesh=mesh, in_specs=placed, out_specs=P(None, None, ("grp", "dev")), check_vma=False
    )

    def whole(*args):
        with jax.sharding.use_abstract_mesh(mesh.abstract_mesh):
            return inner(*args)

    return whole
```

```python
import functools

import jax
import jax.numpy as jnp
from jax import lax
from jax.experimental import pallas as pl
from jax.experimental.pallas import tpu as pltpu
from jax.sharding import PartitionSpec as P

F32 = jnp.float32
BF = jnp.bfloat16
HALO = 16
def halos(first, last, axes):
    count = lax.axis_size(axes)
    up = [(i, i + 1) for i in range(count - 1)]
    down = [(j, i) for i, j in up]
    empty = jnp.zeros_like(first)
    before = lax.ppermute(jnp.concatenate([last, empty], axis=2), axes, up)
    after = lax.ppermute(jnp.concatenate([empty, first], axis=2), axes, down)
    return before, after


NB, LAG, M = 6, 5, 80
STEP = 4


def batcher(n):
    out = []
    p = 1
    while p < n:
        k = p
        while k >= 1:
            for j in range(k % p, n - k, 2 * k):
                for i in range(min(k, n - j - k)):
                    if (i + j) // (2 * p) == (i + j + k) // (2 * p):
                        out.append((i + j, i + j + k))
            k //= 2
        p *= 2
    return out


def take_lanes(ref, row, lane, blk, blocks):
    value = None
    for k in range(blocks):
        t = jnp.take_along_axis(
            ref[row : row + 8, k * 128 : k * 128 + 128], lane, axis=1, mode="promise_in_bounds"
        )
        value = t if value is None else jnp.where(blk == k, t, value)
    return value


def near_setup(rows_ref, pos_ref, mult_ref, count_ref, before_ref, after_ref, near_ref, ext_ref, keys_s, picked, own_s, nacc, cnt_s):
    atoms, leaves = pos_ref.shape[1:]
    width = before_ref.shape[2] // 2
    near_ref[...] = jnp.full_like(near_ref, -1)
    near_ref[0 : rows_ref.shape[0], :] = rows_ref[...]
    ext_ref[...] = jnp.zeros_like(ext_ref)
    for c in range(3):
        ext_ref[32 * c : 32 * c + 32, 0:leaves] = pos_ref[c]
    atom = lax.broadcasted_iota(jnp.int32, (atoms, leaves), 0)
    charge = jnp.where(atom < count_ref[...], mult_ref[...].astype(F32), 0.0)
    ext_ref[96:128, 0:leaves] = charge
    ext_ref[128:136, 0:leaves] = jnp.broadcast_to(count_ref[...].astype(F32), (8, leaves))
    for c in range(4):
        ext_ref[32 * c : 32 * c + 32, leaves : leaves + 2 * width] = before_ref[c] + after_ref[c]
    ext_ref[128:136, leaves : leaves + 2 * width] = before_ref[4, 0:8] + after_ref[4, 0:8]
    blocks = ext_ref.shape[1] // 128
    n_near = picked.shape[1] - 1
    nacc[...] = jnp.zeros_like(nacc)
    for lb in range(2):
        lanes = slice(lb * 128, lb * 128 + 128)
        own_s[lb] = ext_ref[0:96, lanes]
        picked[lb, n_near] = jnp.zeros((128, 128), F32)
        for r in range(0, 32, 8):
            pos = near_ref[r : r + 8, lanes]
            safe = jnp.maximum(pos, 0)
            safe = jnp.where(safe < width, safe + leaves, jnp.where(safe < leaves + width, safe - width, safe))
            count = take_lanes(ext_ref, 128, safe & 127, safe >> 7, blocks)
            keys_s[lb, r : r + 8, :] = jnp.where(pos >= 0, count.astype(jnp.int32) * 512 + safe, 0)
    ks = [keys_s[:, r, :] for r in range(32)]
    for a, b in batcher(32):
        ks[a], ks[b] = jnp.maximum(ks[a], ks[b]), jnp.minimum(ks[a], ks[b])
    total = jnp.int32(0)
    for r in range(32):
        keys_s[:, r, :] = ks[r]
    for r in range(n_near):
        for lb in range(2):
            top = jnp.max(ks[r][lb : lb + 1].astype(F32)).astype(jnp.int32) >> 9
            chunks = (top + STEP - 1) // STEP
            cnt_s[lb, r] = chunks
            total += chunks
    for lb in range(2):
        cnt_s[lb, n_near] = 0

    def gather(n, _):
        for lb in range(2):
            key = jnp.broadcast_to(keys_s[lb, pl.ds(n, 1), :], (8, 128))
            pos = key & 511
            for c in range(4):
                for r in range(0, 32, 8):
                    v = take_lanes(ext_ref, c * 32 + r, pos & 127, pos >> 7, blocks)
                    if c == 3:
                        v = jnp.where(key > 0, v, 0.0)
                    picked[lb, n, c * 32 + r : c * 32 + r + 8, :] = v
        return 0

    lax.fori_loop(0, n_near, gather, 0)
    return total


def near_item(state, picked, own_s, nacc, cnt_s):
    lb, n, k = state
    n_near = picked.shape[1] - 1
    for g in range(4):
        own = [own_s[lb, c * 32 + 8 * g : c * 32 + 8 * g + 8, :] for c in range(3)]
        acc = [nacc[lb, g, i] for i in range(10)]
        for bb in range(STEP):
            src = [picked[lb, n, pl.ds(c * 32 + k * STEP + bb, 1), :] for c in range(4)]
            dx = own[0] - src[0]
            dy = own[1] - src[1]
            dz = own[2] - src[2]
            w = lax.rsqrt(dx * dx + dy * dy + (dz * dz + 0.25))
            w2 = w * w
            qw = src[3] * w
            q3 = qw * w2
            s = q3 * w2
            sx = s * dx
            sy = s * dy
            new = [qw, q3 * dx, q3 * dy, q3 * dz, q3, sx * dx, sy * dy, sx * dy, sx * dz, sy * dz]
            acc = [p + t for p, t in zip(acc, new)]
        for i in range(10):
            nacc[lb, g, i] = acc[i]
    k1 = k + 1
    over = k1 >= cnt_s[lb, n]
    n1 = jnp.where(over, n + 1, n)
    k1 = jnp.where(over, 0, k1)
    out = cnt_s[lb, jnp.minimum(n1, n_near)] == 0
    done = out & (lb == 1)
    lb1 = jnp.where(out, 1, lb)
    n1 = jnp.where(out, jnp.where(done, n_near, 0), n1)
    n1 = jnp.where(cnt_s[lb1, n1] == 0, n_near, n1)
    return lb1, n1, k1


def near_first(cnt_s, n_near):
    lb = jnp.where(cnt_s[0, 0] == 0, 1, 0)
    return lb, jnp.where(cnt_s[lb, 0] == 0, n_near, 0), jnp.int32(0)


def near_finish(near_out, nacc):
    for lb in range(2):
        for g in range(4):
            p, gx, gy, gz, q3, xx, yy, xy, xz, yz = [nacc[lb, g, i] for i in range(10)]
            final = [p, gx, gy, gz, q3 - 3.0 * xx, q3 - 3.0 * yy, -3.0 * xy, -3.0 * xz, -3.0 * yz]
            for c in range(9):
                near_out[c, 8 * g : 8 * g + 8, lb * 128 : lb * 128 + 128] = final[c]


def near_kernel(
    rows_ref, pos_ref, mult_ref, count_ref, before_ref, after_ref, near_out,
    near_s, ext_s, keys_s, picked, own_s, nacc, cnt_s
):
    n_near = picked.shape[1] - 1
    total = near_setup(
        rows_ref, pos_ref, mult_ref, count_ref, before_ref, after_ref, near_s, ext_s, keys_s, picked, own_s, nacc, cnt_s
    )
    first = near_first(cnt_s, n_near)
    lax.fori_loop(0, total, lambda _, st: near_item(st, picked, own_s, nacc, cnt_s), first)
    near_finish(near_out, nacc)


def near(near_rows, pos, charges, counts, before, after):
    n_near = near_rows.shape[0]
    V = pltpu.VMEM
    vm = pl.BlockSpec(memory_space=V)
    return pl.pallas_call(
        near_kernel,
        out_shape=jax.ShapeDtypeStruct((9, 32, 256), F32),
        in_specs=[vm] * 6,
        out_specs=vm,
        scratch_shapes=[
            V((32, 256), jnp.int32),
            V((136, 384), F32),
            V((2, 32, 128), jnp.int32),
            V((2, n_near + 1, 128, 128), F32),
            V((2, 96, 128), F32),
            V((2, 4, 10, 8, 128), F32),
            pltpu.SMEM((2, n_near + 1), jnp.int32),
        ],
        compiler_params=pltpu.CompilerParams(vmem_limit_bytes=12 * 1024 * 1024),
        cost_estimate=pl.CostEstimate(flops=250_000_000, bytes_accessed=40_000_000, transcendentals=7_000_000),
    )(near_rows, pos, charges, counts, before, after)


def fields_inner(
    idx_ref, ops_ref, own_ref, inc_ref, out_ref, idx_s, pool, ptmp, xs, t_s, g_s, acc, *ra
):
    n_off, leaves = idx_ref.shape
    coef = ops_ref.shape[0]
    n_pad = idx_s.shape[0]
    full = n_off // 16
    ra = [ra[:NB], ra[NB:]]
    idx_s[...] = jnp.full_like(idx_s, -1)
    idx_s[0:n_off, :] = idx_ref[...]
    ptmp[...] = jnp.zeros_like(ptmp)
    for h in range(5):
        if h == 0:
            ptmp[0:coef, :] = own_ref[...].astype(F32)
        else:
            ptmp[0:coef, :] = inc_ref[(h - 1) * 256 : h * 256, :].astype(F32).T
        for c in range(8):
            pool[c, h * 16 : (h + 1) * 16, :] = ptmp[c * 16 : (c + 1) * 16, :].astype(BF)
    t_s[...] = jnp.zeros_like(t_s)
    g_s[...] = jnp.zeros_like(g_s)
    acc[...] = jnp.zeros_like(acc)
    xs[...] = jnp.zeros_like(xs)
    xs[0 : coef * 16, 0:coef] = ops_ref[:, 0:16, :].astype(F32).reshape(coef * 16, coef)
    tail = n_off - full * 16
    for k in range(coef):
        xs[4096 + k * 16 : 4096 + k * 16 + tail, 0:coef] = ops_ref[k, full * 16 : n_off, :].astype(F32)
    iota = lax.broadcasted_iota(jnp.int32, (256, 256), 0).astype(F32).astype(BF)
    one = jnp.ones((256, 256), BF)
    zero = jnp.zeros((256, 256), BF)
    half = coef - 64

    def hot(o):
        row = idx_s[pl.ds(o, 1), :]
        lo = jnp.where(row >= 0, row & 255, -1).astype(F32).astype(BF)
        return jnp.where(iota == lo, one, zero)

    def relayout(b):
        c = jnp.minimum(b // 2 + 1, full - 1)
        k0 = lax.rem(b, 2) * half
        to = pl.multiple_of(lax.rem(b // 2 + 1, 2) * 2048 + k0 * 16, 16)
        part = ops_ref[pl.ds(k0, 64), pl.ds(pl.multiple_of(c * 16, 16), 16), :]
        xs[pl.ds(to, 1024), 0:coef] = part.astype(F32).reshape(1024, coef)

    def take_ops(b, w):
        c = b // 2
        slot = jnp.where(c == full, 2, lax.rem(c, 2))
        o8 = lax.rem(b, 2) * 8
        for m in range(2):
            for u in range(2):
                x = xs[pl.ds(slot * 2048 + o8 + 4 * w + 2 * m + u, 128, stride=16), :]
                t_s[w, m, 0:128, 128 * u : 128 * u + 128] = x.astype(BF).T

    def pop_dot1(m, slot, u, c, o, buf):
        r = pltpu.matmul_pop(buf)
        hi = idx_s[pl.ds(o, 1), :] >> 8
        g = r[0:16]
        for h in range(1, 5):
            g = jnp.where(hi == h, r[16 * h : 16 * h + 16], g)
        g_s[slot, m, u * 128 + c * 16 : u * 128 + (c + 1) * 16, :] = g.astype(BF)

    def pop_dot2(m, part, buf):
        acc[m, part * M : (part + 1) * M, :] += pltpu.matmul_pop(buf)

    seq = [("a", 0, c) for c in range(8)] + [("d", 0, 0), ("d", 0, 1)] + [("a", 1, c) for c in range(8)]

    def pop(m, w, item, base, buf):
        kind, u, c = item
        if kind == "a":
            pop_dot1(m, w, u, c, base + 2 * m + u, buf)
        else:
            pop_dot2(m, c, buf)

    def issue(w, s):
        kind, u, c = seq[s]
        for m in range(2):
            buf = ra[m][s % NB]
            if kind == "a":
                pltpu.matmul_acc_lhs(buf, pool[c], load_staged_rhs=0 if c == 0 else None)
            else:
                pltpu.matmul_acc_lhs(buf, t_s[1 - w, m, c * M : (c + 1) * M, :], load_staged_rhs=1 if c == 0 else None)

    n_body = n_pad // 8
    for m in range(2):
        pltpu.matmul_push_rhs(hot(2 * m), 0, m)
    for m in range(2):
        pltpu.matmul_push_rhs(zero, 1, m)
        for s in range(len(seq) - LAG, len(seq)):
            pltpu.matmul_acc_lhs(ra[m][s % NB], pool[0], load_staged_rhs=1 if s == len(seq) - LAG else None)

    def body(b, _):
        for w in range(2):
            base = b * 8 + 4 * w
            prev = jnp.maximum(base - 4, 0)
            for s in range(len(seq)):
                issue(w, s)
                if s == 0:
                    for m in range(2):
                        pltpu.matmul_push_rhs(hot(base + 2 * m + 1), 0, m)
                if s == LAG:
                    for m in range(2):
                        pltpu.matmul_push_rhs(g_s[1 - w, m], 1, m)
                if s == 10:
                    for m in range(2):
                        pltpu.matmul_push_rhs(hot(jnp.minimum(base + 4 + 2 * m, n_pad - 1)), 0, m)
                p = s - LAG
                for m in range(2):
                    if p >= 0:
                        pop(m, w, seq[p], base, ra[m][p % NB])
                    else:
                        pop(m, 1 - w, seq[p + len(seq)], prev, ra[m][(p + len(seq)) % NB])
                if s == 11:
                    take_ops(b, w)
        relayout(b)
        return 0

    lax.fori_loop(0, n_body, body, 0)
    for s in range(len(seq) - LAG, len(seq)):
        for m in range(2):
            pop(m, 1, seq[s], n_pad - 4, ra[m][s % NB])
    for m in range(2):
        pltpu.matmul_acc_lhs(ra[m][0], pool[0], load_staged_rhs=0)
    for m in range(2):
        pltpu.matmul_pop(ra[m][0])
    for m in range(2):
        pltpu.matmul_push_rhs(g_s[1, m], 1, m)
        for c in range(2):
            pltpu.matmul_acc_lhs(ra[m][c], t_s[1, m, c * M : (c + 1) * M, :], load_staged_rhs=1 if c == 0 else None)
    for m in range(2):
        for c in range(2):
            pop_dot2(m, c, ra[m][c])
    out_ref[...] = acc[0, 0:coef, :] + acc[1, 0:coef, :]


def m2l_kernel(*refs):
    accs = [pltpu.ACC(m)((M, 256), F32) for m in range(2) for _ in range(NB)]
    pl.run_scoped(functools.partial(fields_inner, *refs), *accs)


def far_kernel(local_ref, near_ref, field_ref, harm_ref, count_ref, out_ref, der):
    coef = local_ref.shape[0]
    local = local_ref[...]
    for c in range(9):
        d = jnp.dot(field_ref[c], local, precision=lax.Precision.HIGHEST, preferred_element_type=F32)
        d = d.astype(BF).astype(F32)
        for lb in range(2):
            der[lb, c * 128 : c * 128 + coef, :] = d[:, lb * 128 : lb * 128 + 128]
    for lb in range(2):
        lanes = slice(lb * 128, lb * 128 + 128)
        for a0 in range(0, 32, 16):
            start = tuple(near_ref[c, a0 + 8 * g : a0 + 8 * g + 8, lanes] for c in range(9) for g in range(2))

            def add(i, sums):
                sums = list(sums)
                for u in range(11):
                    k = i * 11 + u
                    h = harm_ref[k, a0 : a0 + 16, lanes].astype(F32)
                    for c in range(9):
                        d = der[lb, pl.ds(c * 128 + k, 1), :]
                        for g in range(2):
                            sums[2 * c + g] = sums[2 * c + g] + d * h[8 * g : 8 * g + 8]
                return tuple(sums)

            sums = lax.fori_loop(0, coef // 11, add, start)
            for g in range(2):
                atom = lax.broadcasted_iota(jnp.int32, (8, 128), 0) + (a0 + 8 * g)
                present = atom < count_ref[0:1, lanes]
                for c in range(9):
                    out_ref[c, a0 + 8 * g : a0 + 8 * g + 8, lanes] = jnp.where(present, sums[2 * c + g], 0.0)


def fields_of(idx, ops, own, inc, near_part, field_ops, harmonics, counts):
    n_off = idx.shape[0]
    coef = ops.shape[0]
    n_pad = -(-n_off // 8) * 8
    V = pltpu.VMEM
    vm = pl.BlockSpec(memory_space=V)
    local = pl.pallas_call(
        m2l_kernel,
        out_shape=jax.ShapeDtypeStruct((coef, 256), F32),
        in_specs=[vm] * 4,
        out_specs=vm,
        scratch_shapes=[
            V((n_pad, 256), jnp.int32),
            V((8, M, 256), BF),
            V((128, 256), F32),
            V((3 * 2048, 128), F32),
            V((2, 2, 2 * M, 256), BF),
            V((2, 2, 256, 256), BF),
            V((2, 2 * M, 256), F32),
        ],
        compiler_params=pltpu.CompilerParams(vmem_limit_bytes=24 * 1024 * 1024),
        cost_estimate=pl.CostEstimate(flops=30_000_000_000, bytes_accessed=12_000_000, transcendentals=0),
    )(idx, ops, own, inc)
    return pl.pallas_call(
        far_kernel,
        out_shape=jax.ShapeDtypeStruct((9, 32, 256), F32),
        in_specs=[vm] * 5,
        out_specs=vm,
        scratch_shapes=[V((2, 9 * 128, 128), F32)],
        compiler_params=pltpu.CompilerParams(vmem_limit_bytes=24 * 1024 * 1024),
        cost_estimate=pl.CostEstimate(flops=500_000_000, bytes_accessed=5_000_000, transcendentals=0),
    )(local, near_part, field_ops, harmonics, counts)


def moments_kernel(mult_ref, harm_ref, count_ref, ops_ref, send_ref, mom_ref, out_ref, src, rows_s):
    comps, atoms, _ = mult_ref.shape
    coef = harm_ref.shape[0]
    src[...] = jnp.zeros_like(src)
    for lb in range(2):
        lanes = slice(lb * 128, lb * 128 + 128)
        held = []
        for c in range(comps):
            for g in range(atoms // 16):
                atom = lax.broadcasted_iota(jnp.int32, (16, 128), 0) + 16 * g
                value = mult_ref[c, 16 * g : 16 * g + 16, lanes].astype(F32)
                held.append(jnp.where(atom < count_ref[0:1, lanes], value, 0.0))

        def add(i, held):
            for u in range(11):
                k = i * 11 + u
                h = harm_ref[k, :, lanes].astype(F32)
                for c in range(comps):
                    part = held[2 * c] * h[0:16] + held[2 * c + 1] * h[16:32]
                    src[lb, pl.ds(c * 128 + k, 1), :] = jnp.sum(part[0:8] + part[8:16], axis=0, keepdims=True)
            return held

        lax.fori_loop(0, coef // 11, add, tuple(held))
    mom = jnp.zeros((coef, 256), F32)
    for c in range(comps):
        s = jnp.concatenate([src[lb, c * 128 : c * 128 + coef, :] for lb in range(2)], axis=1)
        mom += lax.dot_general(
            ops_ref[c], s, (((0,), (0,)), ((), ())), precision=lax.Precision.HIGHEST, preferred_element_type=F32
        )
    mom = mom.astype(BF)
    mom_ref[...] = mom
    leaf = lax.broadcasted_iota(jnp.int32, (256, 256), 0)
    slots = send_ref.shape[0]
    rows_s[...] = jnp.zeros_like(rows_s)
    for i in range(slots):
        hot = jnp.where(leaf == send_ref[i : i + 1, :], 1.0, 0.0).astype(BF)
        picked = jnp.dot(mom, hot, preferred_element_type=F32)
        rows_s[pl.ds(i, 256, stride=slots), 0:128] = jnp.pad(picked, ((0, 128 - coef), (0, 0))).T
    out_ref[...] = rows_s[:, 0:coef].astype(BF)


def moments_of(multipoles, harmonics, counts, source_ops, send_rows):
    coef = harmonics.shape[0]
    V = pltpu.VMEM
    vm = pl.BlockSpec(memory_space=V)
    peers = send_rows.shape[1] * send_rows.shape[0]
    return pl.pallas_call(
        moments_kernel,
        out_shape=(jax.ShapeDtypeStruct((coef, 256), BF), jax.ShapeDtypeStruct((peers, coef), BF)),
        in_specs=[vm] * 5,
        out_specs=(vm, vm),
        scratch_shapes=[V((2, 9 * 128, 128), F32), V((peers, 128), F32)],
        compiler_params=pltpu.CompilerParams(vmem_limit_bytes=58 * 1024 * 1024),
        cost_estimate=pl.CostEstimate(flops=500_000_000, bytes_accessed=5_000_000, transcendentals=0),
    )(multipoles, harmonics, counts, source_ops, send_rows)


def shards(
    multipoles,
    harmonics,
    positions,
    atom_counts,
    source_ops,
    field_ops,
    m2l_ops,
    send_list,
    m2l_list,
    near_list,
):
    axes = ("grp", "dev")
    atoms, leaves = positions.shape[1:]
    def ends(cut):
        count = atom_counts[cut][None, :]
        slot = lax.broadcasted_iota(jnp.int32, (atoms, HALO), 0)
        charge = jnp.where(slot < count, multipoles[0, :, cut].astype(F32), 0.0)
        filled = jnp.broadcast_to(count.astype(F32), (atoms, HALO))
        return jnp.concatenate([positions[:, :, cut], charge[None], filled[None]], axis=0)

    before, after = halos(ends(slice(0, HALO)), ends(slice(leaves - HALO, leaves)), axes)
    counts_row = atom_counts.reshape(1, leaves)
    moments, outgoing = moments_of(multipoles, harmonics, counts_row, source_ops, send_list[0].T)
    peer_count, slot_count = send_list.shape[1:]
    coef_count = moments.shape[0]
    outgoing = outgoing.reshape(peer_count, slot_count, coef_count)
    outgoing, before, after = lax.optimization_barrier((outgoing, before, after))
    arrived = lax.all_to_all(outgoing, axes, split_axis=0, concat_axis=0, tiled=True)
    incoming = arrived.reshape(peer_count * slot_count, coef_count)
    near_part = near(near_list, positions, multipoles[0], counts_row, before, after)
    return fields_of(
        m2l_list, m2l_ops.transpose(1, 0, 2), moments, incoming, near_part, field_ops, harmonics, counts_row
    )


def solution(mesh):
    placed = (
        P(None, None, ("grp", "dev")),
        P(None, None, ("grp", "dev")),
        P(None, None, ("grp", "dev")),
        P(("grp", "dev")),
        P(),
        P(),
        P(),
        P(("grp", "dev"), None, None),
        P(None, ("grp", "dev")),
        P(None, ("grp", "dev")),
    )
    inner = jax.shard_map(
        shards, mesh=mesh, in_specs=placed, out_specs=P(None, None, ("grp", "dev")), check_vma=False
    )

    def whole(*args):
        with jax.sharding.use_abstract_mesh(mesh.abstract_mesh):
            return inner(*args)

    return whole
```

```python
import functools

import jax
import jax.numpy as jnp
from jax import lax
from jax.experimental import pallas as pl
from jax.experimental.pallas import tpu as pltpu
from jax.sharding import PartitionSpec as P

F32 = jnp.float32
BF = jnp.bfloat16
HALO = 16
def halos(first, last, axes):
    count = lax.axis_size(axes)
    up = [(i, i + 1) for i in range(count - 1)]
    down = [(j, i) for i, j in up]
    empty = jnp.zeros_like(first)
    before = lax.ppermute(jnp.concatenate([last, empty], axis=2), axes, up)
    after = lax.ppermute(jnp.concatenate([empty, first], axis=2), axes, down)
    return before, after


NB, LAG, M = 6, 5, 80
STEP = 4


def batcher(n):
    out = []
    p = 1
    while p < n:
        k = p
        while k >= 1:
            for j in range(k % p, n - k, 2 * k):
                for i in range(min(k, n - j - k)):
                    if (i + j) // (2 * p) == (i + j + k) // (2 * p):
                        out.append((i + j, i + j + k))
            k //= 2
        p *= 2
    return out


def take_lanes(ref, row, lane, blk, blocks):
    value = None
    for k in range(blocks):
        t = jnp.take_along_axis(
            ref[row : row + 8, k * 128 : k * 128 + 128], lane, axis=1, mode="promise_in_bounds"
        )
        value = t if value is None else jnp.where(blk == k, t, value)
    return value


def near_setup(rows_ref, pos_ref, mult_ref, count_ref, before_ref, after_ref, near_ref, ext_ref, keys_s, picked, own_s, nacc, cnt_s):
    atoms, leaves = pos_ref.shape[1:]
    width = before_ref.shape[2] // 2
    near_ref[...] = jnp.full_like(near_ref, -1)
    near_ref[0 : rows_ref.shape[0], :] = rows_ref[...]
    ext_ref[...] = jnp.zeros_like(ext_ref)
    for c in range(3):
        ext_ref[32 * c : 32 * c + 32, 0:leaves] = pos_ref[c]
    atom = lax.broadcasted_iota(jnp.int32, (atoms, leaves), 0)
    charge = jnp.where(atom < count_ref[...], mult_ref[0].astype(F32), 0.0)
    ext_ref[96:128, 0:leaves] = charge
    ext_ref[128:136, 0:leaves] = jnp.broadcast_to(count_ref[...].astype(F32), (8, leaves))
    for c in range(4):
        ext_ref[32 * c : 32 * c + 32, leaves : leaves + 2 * width] = before_ref[c] + after_ref[c]
    ext_ref[128:136, leaves : leaves + 2 * width] = before_ref[4, 0:8] + after_ref[4, 0:8]
    blocks = ext_ref.shape[1] // 128
    n_near = picked.shape[1] - 1
    nacc[...] = jnp.zeros_like(nacc)
    for lb in range(2):
        lanes = slice(lb * 128, lb * 128 + 128)
        own_s[lb] = ext_ref[0:96, lanes]
        picked[lb, n_near] = jnp.zeros((128, 128), F32)
        for r in range(0, 32, 8):
            pos = near_ref[r : r + 8, lanes]
            safe = jnp.maximum(pos, 0)
            safe = jnp.where(safe < width, safe + leaves, jnp.where(safe < leaves + width, safe - width, safe))
            count = take_lanes(ext_ref, 128, safe & 127, safe >> 7, blocks)
            keys_s[lb, r : r + 8, :] = jnp.where(pos >= 0, count.astype(jnp.int32) * 512 + safe, 0)
    ks = [keys_s[:, r, :] for r in range(32)]
    for a, b in batcher(32):
        ks[a], ks[b] = jnp.maximum(ks[a], ks[b]), jnp.minimum(ks[a], ks[b])
    total = jnp.int32(0)
    for r in range(32):
        keys_s[:, r, :] = ks[r]
    for r in range(n_near):
        for lb in range(2):
            top = jnp.max(ks[r][lb : lb + 1].astype(F32)).astype(jnp.int32) >> 9
            chunks = (top + STEP - 1) // STEP
            cnt_s[lb, r] = chunks
            total += chunks
    for lb in range(2):
        cnt_s[lb, n_near] = 0

    def gather(n, _):
        for lb in range(2):
            key = jnp.broadcast_to(keys_s[lb, pl.ds(n, 1), :], (8, 128))
            pos = key & 511
            for c in range(4):
                for r in range(0, 32, 8):
                    v = take_lanes(ext_ref, c * 32 + r, pos & 127, pos >> 7, blocks)
                    if c == 3:
                        v = jnp.where(key > 0, v, 0.0)
                    picked[lb, n, c * 32 + r : c * 32 + r + 8, :] = v
        return 0

    lax.fori_loop(0, n_near, gather, 0)
    return total


def near_item(state, picked, own_s, nacc, cnt_s):
    lb, n, k = state
    n_near = picked.shape[1] - 1
    for g in range(4):
        own = [own_s[lb, c * 32 + 8 * g : c * 32 + 8 * g + 8, :] for c in range(3)]
        acc = [nacc[lb, g, i] for i in range(10)]
        for bb in range(STEP):
            src = [picked[lb, n, pl.ds(c * 32 + k * STEP + bb, 1), :] for c in range(4)]
            dx = own[0] - src[0]
            dy = own[1] - src[1]
            dz = own[2] - src[2]
            w = lax.rsqrt(dx * dx + dy * dy + (dz * dz + 0.25))
            w2 = w * w
            qw = src[3] * w
            q3 = qw * w2
            s = q3 * w2
            sx = s * dx
            sy = s * dy
            new = [qw, q3 * dx, q3 * dy, q3 * dz, q3, sx * dx, sy * dy, sx * dy, sx * dz, sy * dz]
            acc = [p + t for p, t in zip(acc, new)]
        for i in range(10):
            nacc[lb, g, i] = acc[i]
    k1 = k + 1
    over = k1 >= cnt_s[lb, n]
    n1 = jnp.where(over, n + 1, n)
    k1 = jnp.where(over, 0, k1)
    out = cnt_s[lb, jnp.minimum(n1, n_near)] == 0
    done = out & (lb == 1)
    lb1 = jnp.where(out, 1, lb)
    n1 = jnp.where(out, jnp.where(done, n_near, 0), n1)
    n1 = jnp.where(cnt_s[lb1, n1] == 0, n_near, n1)
    return lb1, n1, k1


def near_first(cnt_s, n_near):
    lb = jnp.where(cnt_s[0, 0] == 0, 1, 0)
    return lb, jnp.where(cnt_s[lb, 0] == 0, n_near, 0), jnp.int32(0)


def near_finish(near_out, nacc):
    for lb in range(2):
        for g in range(4):
            p, gx, gy, gz, q3, xx, yy, xy, xz, yz = [nacc[lb, g, i] for i in range(10)]
            final = [p, gx, gy, gz, q3 - 3.0 * xx, q3 - 3.0 * yy, -3.0 * xy, -3.0 * xz, -3.0 * yz]
            for c in range(9):
                near_out[c, 8 * g : 8 * g + 8, lb * 128 : lb * 128 + 128] = final[c]


def near_kernel(
    rows_ref, pos_ref, mult_ref, count_ref, before_ref, after_ref, near_out,
    near_s, ext_s, keys_s, picked, own_s, nacc, cnt_s
):
    n_near = picked.shape[1] - 1
    total = near_setup(
        rows_ref, pos_ref, mult_ref, count_ref, before_ref, after_ref, near_s, ext_s, keys_s, picked, own_s, nacc, cnt_s
    )
    first = near_first(cnt_s, n_near)
    lax.fori_loop(0, total, lambda _, st: near_item(st, picked, own_s, nacc, cnt_s), first)
    near_finish(near_out, nacc)


def near(near_rows, pos, multipoles, counts, before, after):
    n_near = near_rows.shape[0]
    V = pltpu.VMEM
    vm = pl.BlockSpec(memory_space=V)
    return pl.pallas_call(
        near_kernel,
        out_shape=jax.ShapeDtypeStruct((9, 32, 256), F32),
        in_specs=[vm] * 6,
        out_specs=vm,
        scratch_shapes=[
            V((32, 256), jnp.int32),
            V((136, 384), F32),
            V((2, 32, 128), jnp.int32),
            V((2, n_near + 1, 128, 128), F32),
            V((2, 96, 128), F32),
            V((2, 4, 10, 8, 128), F32),
            pltpu.SMEM((2, n_near + 1), jnp.int32),
        ],
        compiler_params=pltpu.CompilerParams(vmem_limit_bytes=58 * 1024 * 1024),
        cost_estimate=pl.CostEstimate(flops=250_000_000, bytes_accessed=40_000_000, transcendentals=7_000_000),
    )(near_rows, pos, multipoles, counts, before, after)


def fields_inner(
    idx_ref, ops_ref, own_ref, inc_ref, out_ref, idx_s, pool, ptmp, xs, t_s, g_s, acc, *ra
):
    n_off, leaves = idx_ref.shape
    coef = ops_ref.shape[0]
    n_pad = idx_s.shape[0]
    full = n_off // 16
    ra = [ra[:NB], ra[NB:]]
    idx_s[...] = jnp.full_like(idx_s, -1)
    idx_s[0:n_off, :] = idx_ref[...]
    ptmp[...] = jnp.zeros_like(ptmp)
    for h in range(5):
        if h == 0:
            ptmp[0:coef, :] = own_ref[...].astype(F32)
        else:
            ptmp[0:coef, :] = inc_ref[(h - 1) * 256 : h * 256, :].astype(F32).T
        for c in range(8):
            pool[c, h * 16 : (h + 1) * 16, :] = ptmp[c * 16 : (c + 1) * 16, :].astype(BF)
    t_s[...] = jnp.zeros_like(t_s)
    g_s[...] = jnp.zeros_like(g_s)
    acc[...] = jnp.zeros_like(acc)
    xs[...] = jnp.zeros_like(xs)
    xs[0 : coef * 16, 0:coef] = ops_ref[:, 0:16, :].astype(F32).reshape(coef * 16, coef)
    tail = n_off - full * 16
    for k in range(coef):
        xs[4096 + k * 16 : 4096 + k * 16 + tail, 0:coef] = ops_ref[k, full * 16 : n_off, :].astype(F32)
    iota = lax.broadcasted_iota(jnp.int32, (256, 256), 0).astype(F32).astype(BF)
    one = jnp.ones((256, 256), BF)
    zero = jnp.zeros((256, 256), BF)
    half = coef - 64

    def hot(o):
        row = idx_s[pl.ds(o, 1), :]
        lo = jnp.where(row >= 0, row & 255, -1).astype(F32).astype(BF)
        return jnp.where(iota == lo, one, zero)

    def relayout(b):
        c = jnp.minimum(b // 2 + 1, full - 1)
        k0 = lax.rem(b, 2) * half
        to = pl.multiple_of(lax.rem(b // 2 + 1, 2) * 2048 + k0 * 16, 16)
        part = ops_ref[pl.ds(k0, 64), pl.ds(pl.multiple_of(c * 16, 16), 16), :]
        xs[pl.ds(to, 1024), 0:coef] = part.astype(F32).reshape(1024, coef)

    def take_ops(b, w):
        c = b // 2
        slot = jnp.where(c == full, 2, lax.rem(c, 2))
        o8 = lax.rem(b, 2) * 8
        for m in range(2):
            for u in range(2):
                x = xs[pl.ds(slot * 2048 + o8 + 4 * w + 2 * m + u, 128, stride=16), :]
                t_s[w, m, 0:128, 128 * u : 128 * u + 128] = x.astype(BF).T

    def pop_dot1(m, slot, u, c, o, buf):
        r = pltpu.matmul_pop(buf)
        hi = idx_s[pl.ds(o, 1), :] >> 8
        g = r[0:16]
        for h in range(1, 5):
            g = jnp.where(hi == h, r[16 * h : 16 * h + 16], g)
        g_s[slot, m, u * 128 + c * 16 : u * 128 + (c + 1) * 16, :] = g.astype(BF)

    def pop_dot2(m, part, buf):
        acc[m, part * M : (part + 1) * M, :] += pltpu.matmul_pop(buf)

    seq = [("a", 0, c) for c in range(8)] + [("d", 0, 0), ("d", 0, 1)] + [("a", 1, c) for c in range(8)]

    def pop(m, w, item, base, buf):
        kind, u, c = item
        if kind == "a":
            pop_dot1(m, w, u, c, base + 2 * m + u, buf)
        else:
            pop_dot2(m, c, buf)

    def issue(w, s):
        kind, u, c = seq[s]
        for m in range(2):
            buf = ra[m][s % NB]
            if kind == "a":
                pltpu.matmul_acc_lhs(buf, pool[c], load_staged_rhs=0 if c == 0 else None)
            else:
                pltpu.matmul_acc_lhs(buf, t_s[1 - w, m, c * M : (c + 1) * M, :], load_staged_rhs=1 if c == 0 else None)

    n_body = n_pad // 8
    for m in range(2):
        pltpu.matmul_push_rhs(hot(2 * m), 0, m)
    for m in range(2):
        pltpu.matmul_push_rhs(zero, 1, m)
        for s in range(len(seq) - LAG, len(seq)):
            pltpu.matmul_acc_lhs(ra[m][s % NB], pool[0], load_staged_rhs=1 if s == len(seq) - LAG else None)

    def body(b, _):
        for w in range(2):
            base = b * 8 + 4 * w
            prev = jnp.maximum(base - 4, 0)
            for s in range(len(seq)):
                issue(w, s)
                if s == 0:
                    for m in range(2):
                        pltpu.matmul_push_rhs(hot(base + 2 * m + 1), 0, m)
                if s == LAG:
                    for m in range(2):
                        pltpu.matmul_push_rhs(g_s[1 - w, m], 1, m)
                if s == 10:
                    for m in range(2):
                        pltpu.matmul_push_rhs(hot(jnp.minimum(base + 4 + 2 * m, n_pad - 1)), 0, m)
                p = s - LAG
                for m in range(2):
                    if p >= 0:
                        pop(m, w, seq[p], base, ra[m][p % NB])
                    else:
                        pop(m, 1 - w, seq[p + len(seq)], prev, ra[m][(p + len(seq)) % NB])
                if s == 11:
                    take_ops(b, w)
        relayout(b)
        return 0

    lax.fori_loop(0, n_body, body, 0)
    for s in range(len(seq) - LAG, len(seq)):
        for m in range(2):
            pop(m, 1, seq[s], n_pad - 4, ra[m][s % NB])
    for m in range(2):
        pltpu.matmul_acc_lhs(ra[m][0], pool[0], load_staged_rhs=0)
    for m in range(2):
        pltpu.matmul_pop(ra[m][0])
    for m in range(2):
        pltpu.matmul_push_rhs(g_s[1, m], 1, m)
        for c in range(2):
            pltpu.matmul_acc_lhs(ra[m][c], t_s[1, m, c * M : (c + 1) * M, :], load_staged_rhs=1 if c == 0 else None)
    for m in range(2):
        for c in range(2):
            pop_dot2(m, c, ra[m][c])
    out_ref[...] = acc[0, 0:coef, :] + acc[1, 0:coef, :]


def m2l_kernel(*refs):
    accs = [pltpu.ACC(m)((M, 256), F32) for m in range(2) for _ in range(NB)]
    pl.run_scoped(functools.partial(fields_inner, *refs), *accs)


def far_kernel(local_ref, near_ref, field_ref, harm_ref, count_ref, out_ref, der):
    coef = local_ref.shape[0]
    local = local_ref[...]
    for c in range(9):
        d = jnp.dot(field_ref[c], local, precision=lax.Precision.HIGHEST, preferred_element_type=F32)
        d = d.astype(BF).astype(F32)
        for lb in range(2):
            der[lb, c * 128 : c * 128 + coef, :] = d[:, lb * 128 : lb * 128 + 128]
    for lb in range(2):
        lanes = slice(lb * 128, lb * 128 + 128)
        for a0 in range(0, 32, 16):
            start = tuple(near_ref[c, a0 + 8 * g : a0 + 8 * g + 8, lanes] for c in range(9) for g in range(2))

            def add(i, sums):
                sums = list(sums)
                for u in range(11):
                    k = i * 11 + u
                    h = harm_ref[k, a0 : a0 + 16, lanes].astype(F32)
                    for c in range(9):
                        d = der[lb, pl.ds(c * 128 + k, 1), :]
                        for g in range(2):
                            sums[2 * c + g] = sums[2 * c + g] + d * h[8 * g : 8 * g + 8]
                return tuple(sums)

            sums = lax.fori_loop(0, coef // 11, add, start)
            for g in range(2):
                atom = lax.broadcasted_iota(jnp.int32, (8, 128), 0) + (a0 + 8 * g)
                present = atom < count_ref[0:1, lanes]
                for c in range(9):
                    out_ref[c, a0 + 8 * g : a0 + 8 * g + 8, lanes] = jnp.where(present, sums[2 * c + g], 0.0)


def fields_of(idx, ops, own, inc, near_part, field_ops, harmonics, counts):
    n_off = idx.shape[0]
    coef = ops.shape[0]
    n_pad = -(-n_off // 8) * 8
    V = pltpu.VMEM
    vm = pl.BlockSpec(memory_space=V)
    local = pl.pallas_call(
        m2l_kernel,
        out_shape=jax.ShapeDtypeStruct((coef, 256), F32),
        in_specs=[vm] * 4,
        out_specs=vm,
        scratch_shapes=[
            V((n_pad, 256), jnp.int32),
            V((8, M, 256), BF),
            V((128, 256), F32),
            V((3 * 2048, 128), F32),
            V((2, 2, 2 * M, 256), BF),
            V((2, 2, 256, 256), BF),
            V((2, 2 * M, 256), F32),
        ],
        compiler_params=pltpu.CompilerParams(vmem_limit_bytes=24 * 1024 * 1024),
        cost_estimate=pl.CostEstimate(flops=30_000_000_000, bytes_accessed=12_000_000, transcendentals=0),
    )(idx, ops, own, inc)
    return pl.pallas_call(
        far_kernel,
        out_shape=jax.ShapeDtypeStruct((9, 32, 256), F32),
        in_specs=[vm] * 5,
        out_specs=vm,
        scratch_shapes=[V((2, 9 * 128, 128), F32)],
        compiler_params=pltpu.CompilerParams(vmem_limit_bytes=24 * 1024 * 1024),
        cost_estimate=pl.CostEstimate(flops=500_000_000, bytes_accessed=5_000_000, transcendentals=0),
    )(local, near_part, field_ops, harmonics, counts)


def moments_kernel(mult_ref, harm_ref, count_ref, ops_ref, send_ref, mom_ref, out_ref, src, rows_s):
    comps, atoms, _ = mult_ref.shape
    coef = harm_ref.shape[0]
    src[...] = jnp.zeros_like(src)
    for lb in range(2):
        lanes = slice(lb * 128, lb * 128 + 128)
        held = []
        for c in range(comps):
            for g in range(atoms // 16):
                atom = lax.broadcasted_iota(jnp.int32, (16, 128), 0) + 16 * g
                value = mult_ref[c, 16 * g : 16 * g + 16, lanes].astype(F32)
                held.append(jnp.where(atom < count_ref[0:1, lanes], value, 0.0))

        def add(i, held):
            for u in range(11):
                k = i * 11 + u
                h = harm_ref[k, :, lanes].astype(F32)
                for c in range(comps):
                    part = held[2 * c] * h[0:16] + held[2 * c + 1] * h[16:32]
                    src[lb, pl.ds(c * 128 + k, 1), :] = jnp.sum(part[0:8] + part[8:16], axis=0, keepdims=True)
            return held

        lax.fori_loop(0, coef // 11, add, tuple(held))
    mom = jnp.zeros((coef, 256), F32)
    for c in range(comps):
        s = jnp.concatenate([src[lb, c * 128 : c * 128 + coef, :] for lb in range(2)], axis=1)
        mom += lax.dot_general(
            ops_ref[c], s, (((0,), (0,)), ((), ())), precision=lax.Precision.HIGHEST, preferred_element_type=F32
        )
    mom = mom.astype(BF)
    mom_ref[...] = mom
    leaf = lax.broadcasted_iota(jnp.int32, (256, 256), 0)
    slots = send_ref.shape[0]
    rows_s[...] = jnp.zeros_like(rows_s)
    for i in range(slots):
        hot = jnp.where(leaf == send_ref[i : i + 1, :], 1.0, 0.0).astype(BF)
        picked = jnp.dot(mom, hot, preferred_element_type=F32)
        rows_s[pl.ds(i, 256, stride=slots), 0:128] = jnp.pad(picked, ((0, 128 - coef), (0, 0))).T
    out_ref[...] = rows_s[:, 0:coef].astype(BF)


def moments_of(multipoles, harmonics, counts, source_ops, send_rows):
    coef = harmonics.shape[0]
    V = pltpu.VMEM
    vm = pl.BlockSpec(memory_space=V)
    peers = send_rows.shape[1] * send_rows.shape[0]
    return pl.pallas_call(
        moments_kernel,
        out_shape=(jax.ShapeDtypeStruct((coef, 256), BF), jax.ShapeDtypeStruct((peers, coef), BF)),
        in_specs=[vm] * 5,
        out_specs=(vm, vm),
        scratch_shapes=[V((2, 9 * 128, 128), F32), V((peers, 128), F32)],
        compiler_params=pltpu.CompilerParams(vmem_limit_bytes=58 * 1024 * 1024),
        cost_estimate=pl.CostEstimate(flops=500_000_000, bytes_accessed=5_000_000, transcendentals=0),
    )(multipoles, harmonics, counts, source_ops, send_rows)


def shards(
    multipoles,
    harmonics,
    positions,
    atom_counts,
    source_ops,
    field_ops,
    m2l_ops,
    send_list,
    m2l_list,
    near_list,
):
    axes = ("grp", "dev")
    atoms, leaves = positions.shape[1:]
    def ends(cut):
        count = atom_counts[cut][None, :]
        slot = lax.broadcasted_iota(jnp.int32, (atoms, HALO), 0)
        charge = jnp.where(slot < count, multipoles[0, :, cut].astype(F32), 0.0)
        filled = jnp.broadcast_to(count.astype(F32), (atoms, HALO))
        return jnp.concatenate([positions[:, :, cut], charge[None], filled[None]], axis=0)

    before, after = halos(ends(slice(0, HALO)), ends(slice(leaves - HALO, leaves)), axes)
    counts_row = atom_counts.reshape(1, leaves)
    moments, outgoing = moments_of(multipoles, harmonics, counts_row, source_ops, send_list[0].T)
    peer_count, slot_count = send_list.shape[1:]
    coef_count = moments.shape[0]
    outgoing = outgoing.reshape(peer_count, slot_count, coef_count)
    outgoing, before, after = lax.optimization_barrier((outgoing, before, after))
    arrived = lax.all_to_all(outgoing, axes, split_axis=0, concat_axis=0, tiled=True)
    incoming = arrived.reshape(peer_count * slot_count, coef_count)
    near_part = near(near_list, positions, multipoles, counts_row, before, after)
    return fields_of(
        m2l_list, m2l_ops.transpose(1, 0, 2), moments, incoming, near_part, field_ops, harmonics, counts_row
    )


def solution(mesh):
    placed = (
        P(None, None, ("grp", "dev")),
        P(None, None, ("grp", "dev")),
        P(None, None, ("grp", "dev")),
        P(("grp", "dev")),
        P(),
        P(),
        P(),
        P(("grp", "dev"), None, None),
        P(None, ("grp", "dev")),
        P(None, ("grp", "dev")),
    )
    inner = jax.shard_map(
        shards, mesh=mesh, in_specs=placed, out_specs=P(None, None, ("grp", "dev")), check_vma=False
    )

    def whole(*args):
        with jax.sharding.use_abstract_mesh(mesh.abstract_mesh):
            return inner(*args)

    return whole
```
